32 devices in a mesh: space: 8 (over z, x), rep: 4 (over y, core).
Axes of the slice: x: 2, y: 2, z: 4, core: 2. Of those that a mesh axis runs over, the one named last changes fastest.
Arguments:
- stem_input: bfloat16 [4, 32, 512, 256], P('rep', 'space'), may hold values from -6 to 6
- stem_preact: bfloat16 [4, 16, 256, 256], P('rep', 'space'), may hold values from -6 to 6
- deep_cotangent: bfloat16 [4, 16, 256, 1024], P('rep', None, 'space'), may hold values from -6 to 6
- tissue_tiles: int32 [4], P('rep'), may hold values from 1 to 64
- conv_weight: bfloat16 [3, 3, 256, 256], replicated, may hold values from -0.125 to 0.125
- expand_weight: bfloat16 [256, 1024], replicated, may hold values from -0.1875 to 0.1875
Outputs:
- grad_input: bfloat16 [4, 32, 512, 256], P('rep', 'space')
- grad_conv: float32 [3, 3, 256, 256], replicated
- grad_expand: float32 [256, 1024], replicated
The draws below stay inside these ranges and needn't reach their ends.
All inputs are finite; a program needn't handle non-finite values.
Results may differ from the reference program's by a relative error of at most 0.001.
The reference program's roundings to bfloat16 on the way (of `weighted`, `active`, `grad_hidden` and `grad_pre`) count: a program that leaves them out, or rounds other values in their place, can miss the bound.
Values may be sent and summed in bfloat16 or wider, within the bound.
A program may use at most 128 MiB of HBM per device.

```python
import jax
import jax.numpy as jnp
from jax import lax

C = 256
CD = 1024
TILES = 64
COLS = 512
SAMPLES = 4
H0 = 32
H1 = 16
OUT_COLS = 256
N_REP = 4


def place_ends(entries, own_key, smallest, top_value):
    longest = entries.shape.index(max(entries.shape))
    spots = []
    for shift in (0, 1):
        where = [jax.random.randint(jax.random.fold_in(own_key, axis), (), 0, length) for axis, length in enumerate(entries.shape)]
        where[longest] = (where[longest] + shift) % entries.shape[longest]
        spots.append(tuple(where))
    return entries.at[spots[0]].set(smallest).at[spots[1]].set(top_value)


def with_spikes(entries, own_key, source, target, parts, factor):
    owner, partner = [(jnp.arange(entries.shape[axis_at]) // (entries.shape[axis_at] // parts)).reshape([-1 if axis == axis_at else 1 for axis in range(entries.ndim)]) for axis_at in (source, target)]
    chosen = jax.random.permutation(own_key, parts)[partner]
    strong = (owner == chosen) | (owner == (partner + parts // 2) % parts)
    return jnp.where(strong, factor * entries, entries)


def levels(rng, extent, shards, least, high):
    def one(axis_at, shards_of):
        heights = jax.random.uniform(jax.random.fold_in(jax.random.fold_in(rng, 6), axis_at), (shards_of,), jnp.float32, least / len(shards), high / len(shards))
        return jnp.repeat(jnp.exp(heights), extent[axis_at] // shards_of).reshape((-1,) + (1,) * (len(extent) - axis_at - 1))

    factor_of = one(*shards[0])
    for cut in shards[1:]:
        factor_of = factor_of * one(*cut)
    return factor_of


def normal_values(stream_key, dims, width, reach, cuts=(), dtype=jnp.bfloat16):
    drawn = jax.random.normal(stream_key, dims, jnp.float32) * width
    if len(cuts) > 0:
        drawn = levels(stream_key, dims, cuts, -0.22, 0.18) * drawn
    return jnp.clip(drawn, min=-reach, max=reach).astype(dtype)


def noise_with(stream_key, shape, spread, most, split, heavy, dtype=jnp.bfloat16):
    drawn = spread * jax.random.normal(stream_key, shape, jnp.float32)
    if split:
        drawn = drawn * levels(stream_key, shape, split, -0.22, 0.18)
    return jnp.clip(with_spikes(drawn, jax.random.fold_in(stream_key, 3), *heavy), -most, most).astype(dtype)


def setup_inputs(seed: int = 0) -> dict:
    keys = jax.random.split(jax.random.key(seed), 7)
    stem_input = normal_values(keys[0], (SAMPLES, H0, COLS, C), 1.0, 6.0, ((0, 4), (1, 8)))
    stem_preact = noise_with(keys[1], (SAMPLES, H1, OUT_COLS, C), 1.0, 6.0, ((0, 4), (1, 8)), (1, 3, 8, 2.0))
    deep_cotangent = noise_with(keys[2], (SAMPLES, H1, OUT_COLS, CD), 1.0, 6.0, ((0, 4), (2, 8)), (2, 3, 8, 2.0))
    tissue_tiles = place_ends(jax.random.randint(keys[3], (SAMPLES,), 1, TILES + 1), jax.random.fold_in(keys[3], 1), 1, TILES).astype(jnp.int32)
    conv_weight = normal_values(keys[4], (3, 3, C, C), (9 * C) ** -0.5, 0.125)
    expand_weight = normal_values(keys[5], (C, CD), CD ** -0.5, 0.1875)
    return dict(stem_input=stem_input, stem_preact=stem_preact, deep_cotangent=deep_cotangent, tissue_tiles=tissue_tiles, conv_weight=conv_weight, expand_weight=expand_weight)


def weight_taps(above, strip_rows, cotangent):
    samples_here, half_rows, width_out, channels_out = cotangent.shape
    zero_row = jnp.zeros_like(strip_rows[:, :1])
    padded = jnp.concatenate([above, strip_rows, zero_row], axis=1)
    zero_col = jnp.zeros_like(padded[:, :, :1])
    padded = jnp.concatenate([zero_col, padded, zero_col], axis=2)
    padded = padded.reshape(samples_here, half_rows + 1, 2, width_out + 1, 2, strip_rows.shape[3])
    blocks = []
    for row_tap in range(3):
        for col_tap in range(3):
            window = padded[:, row_tap // 2:row_tap // 2 + half_rows, row_tap % 2, col_tap // 2:col_tap // 2 + width_out, col_tap % 2, :]
            blocks.append(lax.dot_general(window, cotangent, (((0, 1, 2), (0, 1, 2)), ((), ())), preferred_element_type=jnp.float32))
    return jnp.stack(blocks, axis=1)

def input_grad(extended, conv_weight):
    samples_here, ext_rows, width_out, channels_out = extended.shape
    half_rows = ext_rows - 1
    tap_terms = lax.dot_general(extended, conv_weight, (((3,), (3,)), ((), ())), preferred_element_type=jnp.float32)
    accumulated = jnp.zeros((samples_here, half_rows + 1, 2, width_out + 1, 2, conv_weight.shape[2]), jnp.float32)
    for row_tap in range(3):
        if row_tap < 2:
            row_target, row_source, row_parity = (slice(0, half_rows + 1), slice(0, half_rows + 1), row_tap)
        else:
            row_target, row_source, row_parity = (slice(1, half_rows + 1), slice(0, half_rows), 0)
        for col_tap in range(3):
            if col_tap < 2:
                col_target, col_source, col_parity = (slice(0, width_out), slice(0, width_out), col_tap)
            else:
                col_target, col_source, col_parity = (slice(1, width_out + 1), slice(0, width_out), 0)
            accumulated = accumulated.at[:, row_target, row_parity, col_target, col_parity, :].add(tap_terms[:, row_source, col_source, row_tap, col_tap, :])
    accumulated = accumulated.reshape(samples_here, 2 * half_rows + 2, 2 * width_out + 2, conv_weight.shape[2])
    return accumulated[:, 1:2 * half_rows + 1, 1:2 * width_out + 1, :].astype(jnp.bfloat16)

def group_grads(stem_input, stem_preact, deep_cotangent, tissue_tiles, conv_weight, expand_weight):
    tile_share = tissue_tiles.astype(jnp.float32) / TILES
    weighted = (deep_cotangent.astype(jnp.float32) * tile_share[:, None, None, None]).astype(jnp.bfloat16)
    active = jnp.maximum(stem_preact, jnp.zeros_like(stem_preact))
    grad_hidden = lax.dot_general(weighted, expand_weight, (((3,), (1,)), ((), ())), preferred_element_type=jnp.float32).astype(jnp.bfloat16)
    grad_pre = jnp.where(stem_preact > 0, grad_hidden, jnp.zeros_like(grad_hidden))
    part_expand = lax.dot_general(active, weighted, (((0, 1, 2), (0, 1, 2)), ((), ())), preferred_element_type=jnp.float32)
    above = jnp.zeros_like(stem_input[:, :1])
    part_conv = weight_taps(above, stem_input, grad_pre)
    extended = jnp.concatenate([grad_pre, jnp.zeros_like(grad_pre[:, :1])], axis=1)
    grad_input = input_grad(extended, conv_weight)
    return (grad_input, part_conv, part_expand)

def reference(stem_input, stem_preact, deep_cotangent, tissue_tiles, conv_weight, expand_weight):
    groups = N_REP

    def regroup(stacked):
        return stacked.reshape((groups, stacked.shape[0] // groups) + stacked.shape[1:])

    def advance(running, members):
        conv_total, expand_total = running
        grad_part, part_conv, part_expand = group_grads(members[0], members[1], members[2], members[3], conv_weight, expand_weight)
        return ((conv_total + part_conv, expand_total + part_expand), grad_part)
    initial = (jnp.zeros((C, 9, C), jnp.float32), jnp.zeros((C, CD), jnp.float32))
    running, grad_parts = lax.scan(advance, initial, (regroup(stem_input), regroup(stem_preact), regroup(deep_cotangent), regroup(tissue_tiles)))
    grad_scale = float(SAMPLES * H1 * OUT_COLS) ** (-0.5)
    grad_input = grad_parts.reshape(stem_input.shape)
    grad_conv = (running[0] * grad_scale).reshape(C, 3, 3, C).transpose(1, 2, 0, 3)
    grad_expand = running[1] * grad_scale
    return (grad_input, grad_conv, grad_expand)
```

```python
import jax
import jax.numpy as jnp
from jax import lax
from jax.sharding import PartitionSpec as P

TILES = 64


def shifted(x, axis, by):
    length = lax.axis_size(axis)
    pairs = [(i, i + by) for i in range(length) if 0 <= i + by < length]
    return lax.ppermute(x, axis, pairs)


def contract(lhs, rhs):
    return lax.dot_general(
        lhs, rhs, (((0, 1, 2), (0, 1, 2)), ((), ())), preferred_element_type=jnp.float32
    )


def next_column(x):
    return jnp.concatenate([x[:, :, 1:], jnp.zeros_like(x[:, :, :1])], axis=2)


def weight_taps(strip_rows, here, lower):
    samples, rows, cols, channels = strip_rows.shape
    parts = strip_rows.reshape(samples, rows // 2, 2, cols // 2, 2, channels)
    source = {(a, b): parts[:, :, a, :, b] for a in range(2) for b in range(2)}
    taps = []
    for row_tap in range(3):
        grads = lower if row_tap == 0 else here
        for col_tap in range(3):
            grad = next_column(grads) if col_tap == 0 else grads
            taps.append(contract(source[(row_tap + 1) % 2, (col_tap + 1) % 2], grad))
    return jnp.stack(taps, axis=0)


def input_grad(here, lower, conv_weight):
    def term(pieces):
        lhs = jnp.concatenate([grad for grad, _, _ in pieces], axis=3)
        rhs = jnp.concatenate([conv_weight[p, q] for _, p, q in pieces], axis=1)
        out = lax.dot_general(
            lhs, rhs, (((3,), (1,)), ((), ())), preferred_element_type=jnp.float32
        )
        return out.astype(jnp.bfloat16)

    here_next, lower_next = next_column(here), next_column(lower)
    even = [term([(here, 1, 1)]), term([(here, 1, 2), (here_next, 1, 0)])]
    odd = [
        term([(here, 2, 1), (lower, 0, 1)]),
        term([(here, 2, 2), (here_next, 2, 0), (lower, 0, 2), (lower_next, 0, 0)]),
    ]
    both = jnp.stack([jnp.stack(even, axis=3), jnp.stack(odd, axis=3)], axis=2)
    samples, rows, cols, channels = here.shape
    return both.reshape(samples, 2 * rows, 2 * cols, channels)


def body(stem_input, stem_preact, deep_cotangent, tissue_tiles, conv_weight, expand_weight):
    tile_share = tissue_tiles.astype(jnp.float32) / TILES
    weighted = (deep_cotangent.astype(jnp.float32) * tile_share[:, None, None, None]).astype(
        jnp.bfloat16
    )
    hidden_deep = lax.dot_general(
        weighted, expand_weight, (((3,), (1,)), ((), ())), preferred_element_type=jnp.float32
    ).astype(jnp.bfloat16)
    grad_hidden = lax.all_to_all(hidden_deep, "space", split_axis=1, concat_axis=2, tiled=True)
    grad_pre = jnp.where(stem_preact > 0, grad_hidden, jnp.zeros_like(grad_hidden))
    active = jnp.maximum(stem_preact, jnp.zeros_like(stem_preact))
    active_deep = lax.all_to_all(active, "space", split_axis=2, concat_axis=1, tiled=True)
    part_expand = contract(active_deep, weighted)
    below = shifted(grad_pre[:, :1], "space", -1)
    lower = jnp.concatenate([grad_pre[:, 1:], below], axis=1)
    part_conv = weight_taps(stem_input, grad_pre, lower)
    samples_all = stem_input.shape[0] * lax.axis_size("rep")
    rows_all = stem_preact.shape[1] * lax.axis_size("space")
    grad_scale = float(samples_all * rows_all * stem_preact.shape[2]) ** (-0.5)
    channels = conv_weight.shape[2]
    conv_sum, expand_sum = lax.psum((part_conv, part_expand), ("space", "rep"))
    grad_input = input_grad(grad_pre, lower, conv_weight)
    grad_conv = conv_sum.reshape(3, 3, channels, channels) * grad_scale
    return (grad_input, grad_conv, expand_sum * grad_scale)


def solution(mesh):
    return jax.shard_map(
        body,
        mesh=mesh,
        in_specs=(
            P("rep", "space", None, None),
            P("rep", "space", None, None),
            P("rep", None, "space", None),
            P("rep"),
            P(),
            P(),
        ),
        out_specs=(P("rep", "space", None, None), P(), P()),
        check_vma=False,
    )
```

```python
import functools

import jax
import jax.numpy as jnp
from jax import lax
from jax.experimental import pallas as pl
from jax.experimental.pallas import tpu as pltpu
from jax.sharding import PartitionSpec as P

TILES = 64
F32, BF16 = jnp.float32, jnp.bfloat16
LEAD = "core"
ORDERS = (("y", "x"), ("x", "y"), ("y", "x"), ("x", "y"))


def dot(lhs, rhs, lhs_dim, rhs_dim):
    return lax.dot_general(
        lhs, rhs, (((lhs_dim,), (rhs_dim,)), ((), ())), preferred_element_type=F32
    )


def layout(n_space, n_rep):
    n_x = 2 if n_space % 2 == 0 else 1
    n_core = 2 if n_rep % 2 == 0 else 1
    return {"z": n_space // n_x, "x": n_x, "y": n_rep // n_core, "core": n_core}


def padded_rows(rows, n_devices):
    unit = 8 * n_devices
    return -(-rows // unit) * unit


def kernel(
    n_space, n_rep, piece_rows, valid_rows,
    share_ref, x_hbm, pre_ref, cot_ref, cw_hbm, ew_ref,
    gi_hbm, gc_hbm, ge_hbm,
    x_ref, cw_ref, weighted, hid_send, hid_recv, act_send, act_recv,
    spread, taps_in, grads, grads_next, below, gi_ref, mixed,
    acc, landing, total,
    load_sem, store_sem, hid_sems, act_sems, below_sems, rs_send, rs_recv, ag_send, ag_recv,
):
    s, r = lax.axis_index("space"), lax.axis_index("rep")
    sizes = layout(n_space, n_rep)
    n_x, n_core = sizes["x"], sizes["core"]
    here = {"z": s // n_x, "x": s % n_x, "y": r // n_core, "core": r % n_core}
    half_rows, width, channels = pre_ref.shape
    band = width // n_space
    block = half_rows * band

    def peer(axis, at):
        if axis == "z":
            return (at * n_x + here["x"], r)
        if axis == "x":
            return (here["z"] * n_x + at, r)
        if axis == "y":
            return (s, at * n_core + here["core"])
        return (s, here["y"] * n_core + at)

    load_x = pltpu.make_async_copy(x_hbm, x_ref, load_sem.at[0])
    load_cw = pltpu.make_async_copy(cw_hbm, cw_ref, load_sem.at[1])
    load_x.start()
    load_cw.start()

    barrier = pltpu.get_barrier_semaphore()
    partners = [((s + d) % n_space, r) for d in range(1, n_space)]
    for axis in ("y", "core"):
        partners += [peer(axis, (here[axis] + d) % sizes[axis]) for d in range(1, sizes[axis])]
    for partner in partners:
        pl.semaphore_signal(
            barrier, inc=1, device_id=partner, device_id_type=pl.DeviceIdType.MESH
        )

    weighted[...] = (cot_ref[...].astype(F32) * share_ref[0]).astype(BF16)
    hidden = dot(weighted[...], ew_ref[...], 1, 1).astype(BF16)
    for j in range(n_space):
        hid_send[j] = hidden[j * block : (j + 1) * block]
    for j in range(n_space):
        for i in range(half_rows):
            rows = pre_ref[i, j * band : (j + 1) * band, :].astype(F32)
            act_send[j, i * band : (i + 1) * band, :] = jnp.maximum(rows, 0.0).astype(BF16)
    pl.semaphore_wait(barrier, len(partners))

    def exchange(source, target, sems):
        copies = []
        for d in range(1, n_space):
            to = (s + d) % n_space
            copies.append(
                pltpu.make_async_remote_copy(
                    src_ref=source.at[to],
                    dst_ref=target.at[s],
                    send_sem=sems.at[0, d],
                    recv_sem=sems.at[1, d],
                    device_id=(to, r),
                    device_id_type=pl.DeviceIdType.MESH,
                )
            )
            copies[-1].start()
        target[s] = source[s]
        return copies

    hid_copies = exchange(hid_send, hid_recv, hid_sems)
    act_copies = exchange(act_send, act_recv, act_sems)

    out_at = lax.broadcasted_iota(jnp.int32, (2 * width, 2 * width), 0)
    in_at = lax.broadcasted_iota(jnp.int32, (2 * width, 2 * width), 1)
    wanted = jnp.where(in_at < width, 2 * in_at, 2 * (in_at - width) + 1)
    spread[...] = jnp.where(out_at == wanted, 1.0, 0.0).astype(BF16)
    load_x.wait()
    for row in range(2 * half_rows):
        split = dot(x_ref[row], spread[...], 0, 0).astype(BF16)
        at = (row // 2) * width
        for parity in range(2):
            taps_in[row % 2, parity, :, at : at + width] = split[
                :, parity * width : (parity + 1) * width
            ]

    for copy in hid_copies:
        copy.wait()

    column = lax.broadcasted_iota(jnp.int32, (width, channels), 0)

    def put_grad(i, value):
        grads[i * width : (i + 1) * width, :] = value.astype(BF16)
        moved = jnp.where(column < width - 1, pltpu.roll(value, width - 1, 0), 0.0)
        grads_next[i * width : (i + 1) * width, :] = moved.astype(BF16)

    for i in range(half_rows):
        arrived = jnp.concatenate(
            [hid_recv[j, i * band : (i + 1) * band, :].astype(F32) for j in range(n_space)], axis=0
        )
        put_grad(i, jnp.where(pre_ref[i].astype(F32) > 0, arrived, 0.0))
    below_copy = pltpu.make_async_remote_copy(
        src_ref=grads.at[0:width],
        dst_ref=below,
        send_sem=below_sems.at[0],
        recv_sem=below_sems.at[1],
        device_id=((s + n_space - 1) % n_space, r),
        device_id_type=pl.DeviceIdType.MESH,
    )

    @pl.when(s > 0)
    def _():
        below_copy.start()

    starts = [sum(piece_rows[:k]) for k in range(len(piece_rows))]
    span = half_rows * width

    def conv_piece(k, row_tap):
        first = width if row_tap == 0 else 0
        for col_tap in range(3):
            grad = grads_next if col_tap == 0 else grads
            at = starts[k] + col_tap * channels
            acc[at : at + channels, :] = dot(
                taps_in[(row_tap + 1) % 2, (col_tap + 1) % 2], grad[first : first + span, :], 1, 0
            )

    def piece(k):
        if piece_rows[k] > valid_rows[k]:
            acc[starts[k] + valid_rows[k] : starts[k] + piece_rows[k], :] = jnp.zeros(
                (piece_rows[k] - valid_rows[k], acc.shape[1]), F32
            )
        base, length = starts[k], piece_rows[k]
        slot, sem = starts[k], 0
        levels = []
        for axis in (LEAD,) + ORDERS[k] + ("z",):
            n, at = sizes[axis], here[axis]
            if n == 1:
                continue
            sub = length // n
            copies, slots = [], []
            for d in range(1, n):
                to = (at + d) % n
                copies.append(
                    pltpu.make_async_remote_copy(
                        src_ref=acc.at[pl.ds(pl.multiple_of(base + to * sub, 8), sub)],
                        dst_ref=landing.at[pl.ds(slot, sub)],
                        send_sem=rs_send.at[k, sem],
                        recv_sem=rs_recv.at[k, sem],
                        device_id=peer(axis, to),
                        device_id_type=pl.DeviceIdType.MESH,
                    )
                )
                copies[-1].start()
                slots.append(slot)
                slot += sub
                sem += 1
            yield
            for copy in copies:
                copy.wait()
            base = base + at * sub
            own = pl.ds(pl.multiple_of(base, 8), sub)
            value = acc[own, :]
            for place in slots:
                value = value + landing[place : place + sub, :]
            acc[own, :] = value
            length = sub
            levels.append((axis, n, at, base, sub))
        total[own, :] = value
        sem = 0
        for axis, n, at, base, sub in reversed(levels):
            copies = []
            mine = total.at[pl.ds(pl.multiple_of(base, 8), sub)]
            for d in range(1, n):
                copies.append(
                    pltpu.make_async_remote_copy(
                        src_ref=mine,
                        dst_ref=mine,
                        send_sem=ag_send.at[k, sem],
                        recv_sem=ag_recv.at[k, sem],
                        device_id=peer(axis, (at + d) % n),
                        device_id_type=pl.DeviceIdType.MESH,
                    )
                )
                copies[-1].start()
                sem += 1
            yield
            for copy in copies:
                copy.wait()

    pieces = [piece(k) for k in range(4)]
    conv_piece(0, 1)
    next(pieces[0])
    conv_piece(1, 2)
    next(pieces[1])

    @pl.when(s < n_space - 1)
    def _():
        below_copy.wait_recv()

    last = jnp.where(s < n_space - 1, 1.0, 0.0)
    lower = below[...].astype(F32)
    put_grad(half_rows, jnp.where(last > 0.5, lower, 0.0))
    next(pieces[0])
    conv_piece(2, 0)
    next(pieces[2])
    next(pieces[1])
    for copy in act_copies:
        copy.wait()
    active = act_recv[...].astype(F32).reshape(n_space * block, channels).astype(BF16)
    deep = weighted.shape[1]
    for k in range(deep // channels):
        at = starts[3] + k * channels
        acc[at : at + channels, :] = dot(
            active, weighted[:, k * channels : (k + 1) * channels], 0, 0
        )
    next(pieces[3])
    next(pieces[2])
    next(pieces[3])

    load_cw.wait()

    def term(first, row_tap, col_tap):
        grad = grads_next if col_tap == 0 else grads
        return dot(grad[first : first + span, :], cw_ref[row_tap, col_tap], 1, 1)

    stores = []
    for row_parity in range(2):
        pairs = [(0, 1)] if row_parity == 0 else [(0, 2), (width, 0)]
        for parity in range(2):
            cols = (1,) if parity == 0 else (2, 0)
            terms = [term(first, p, q) for first, p in pairs for q in cols]
            mixed[parity] = functools.reduce(jnp.add, terms).astype(BF16)
        for i in range(half_rows):
            both = jnp.concatenate(
                [mixed[parity, i * width : (i + 1) * width, :] for parity in range(2)], axis=0
            )
            row = 2 * i + row_parity
            gi_ref[row] = dot(spread[...], both, 1, 0).astype(BF16)
            stores.append(
                pltpu.make_async_copy(gi_ref.at[row], gi_hbm.at[row], store_sem.at[row])
            )
            stores[-1].start()

    slot = 2 * half_rows
    waiting = list(range(4))
    while waiting:
        for k in list(waiting):
            if next(pieces[k], "end") != "end":
                continue
            waiting.remove(k)
            if k < 3:
                rows = total.at[pl.ds(starts[k], valid_rows[k])]
                outs = [(rows, gc_hbm.at[(1, 2, 0)[k]])]
            else:
                outs = [
                    (
                        total.at[pl.ds(starts[k] + m * channels, channels)],
                        ge_hbm.at[:, pl.ds(m * channels, channels)],
                    )
                    for m in range(deep // channels)
                ]
            for source, target in outs:
                stores.append(pltpu.make_async_copy(source, target, store_sem.at[slot]))
                stores[-1].start()
                slot += 1

    @pl.when(s > 0)
    def _():
        below_copy.wait_send()

    for store in stores:
        store.wait()


def body(n_space, n_rep, stem_input, stem_preact, deep_cotangent, tissue_tiles, conv_weight, expand_weight):
    share = tissue_tiles.astype(F32) / TILES
    _, in_rows, cols, channels = stem_input.shape
    _, half_rows, width, _ = stem_preact.shape
    _, deep_rows, band, deep = deep_cotangent.shape
    devices = n_space * n_rep
    block = half_rows * band
    valid_rows = [3 * channels] * 3 + [deep]
    piece_rows = [padded_rows(rows, devices) for rows in valid_rows]
    all_rows = sum(piece_rows)
    sizes = layout(n_space, n_rep)
    copies = sum(n - 1 for n in sizes.values())
    vmem = pl.BlockSpec(memory_space=pltpu.VMEM)
    anywhere = pl.BlockSpec(memory_space=pl.ANY)
    dma = pltpu.SemaphoreType.DMA
    grad_input, conv_sum, expand_sum = pl.pallas_call(
        functools.partial(kernel, n_space, n_rep, piece_rows, valid_rows),
        out_shape=(
            jax.ShapeDtypeStruct((in_rows, cols, channels), BF16),
            jax.ShapeDtypeStruct((3, 3 * channels, channels), F32),
            jax.ShapeDtypeStruct((channels, deep), F32),
        ),
        in_specs=[
            pl.BlockSpec(memory_space=pltpu.SMEM),
            anywhere,
            vmem,
            vmem,
            anywhere,
            vmem,
        ],
        out_specs=(anywhere, anywhere, anywhere),
        scratch_shapes=[
            pltpu.VMEM((in_rows, cols, channels), BF16),
            pltpu.VMEM(conv_weight.shape, BF16),
            pltpu.VMEM((deep_rows * band, deep), BF16),
            pltpu.VMEM((n_space, block, channels), BF16),
            pltpu.VMEM((n_space, block, channels), BF16),
            pltpu.VMEM((n_space, block, channels), BF16),
            pltpu.VMEM((n_space, block, channels), BF16),
            pltpu.VMEM((cols, cols), BF16),
            pltpu.VMEM((2, 2, channels, half_rows * width), BF16),
            pltpu.VMEM(((half_rows + 1) * width, channels), BF16),
            pltpu.VMEM(((half_rows + 1) * width, channels), BF16),
            pltpu.VMEM((width, channels), BF16),
            pltpu.VMEM((in_rows, cols, channels), BF16),
            pltpu.VMEM((2, half_rows * width, channels), BF16),
            pltpu.VMEM((all_rows, channels), F32),
            pltpu.VMEM((all_rows, channels), F32),
            pltpu.VMEM((all_rows, channels), F32),
            dma((2,)),
            dma((in_rows + 3 + deep // channels,)),
            dma((2, n_space)),
            dma((2, n_space)),
            dma((2,)),
            dma((4, copies)),
            dma((4, copies)),
            dma((4, copies)),
            dma((4, copies)),
        ],
        compiler_params=pltpu.CompilerParams(
            collective_id=0, has_side_effects=True, vmem_limit_bytes=56 * 1024 * 1024
        ),
    )(
        share,
        stem_input[0],
        stem_preact[0],
        deep_cotangent.reshape(deep_rows * band, deep),
        conv_weight,
        expand_weight,
    )
    grad_scale = float(n_rep * half_rows * n_space * width) ** (-0.5)
    grad_conv = conv_sum.reshape(3, 3, channels, channels) * grad_scale
    return (grad_input[None], grad_conv, expand_sum * grad_scale)


def solution(mesh):
    return jax.shard_map(
        functools.partial(body, mesh.shape["space"], mesh.shape["rep"]),
        mesh=mesh,
        in_specs=(
            P("rep", "space", None, None),
            P("rep", "space", None, None),
            P("rep", None, "space", None),
            P("rep"),
            P(),
            P(),
        ),
        out_specs=(P("rep", "space", None, None), P(), P()),
        check_vma=False,
    )
```

```python
import functools
import heapq

import jax
import jax.numpy as jnp
from jax import lax
from jax.experimental import pallas as pl
from jax.experimental.pallas import tpu as pltpu
from jax.sharding import PartitionSpec as P

TILES = 64
VMEM_LIMIT = 32 * 1024 * 1024
F32, BF16 = jnp.float32, jnp.bfloat16
ORDERS = ("xyz", "yxz", "xzy", "yxz", "xyz", "yzx")
UNITS = tuple((p, q) for p in (1, 2, 0) for q in range(3))


def dot(lhs, rhs, lhs_dim, rhs_dim):
    return lax.dot_general(
        lhs, rhs, (((lhs_dim,), (rhs_dim,)), ((), ())), preferred_element_type=F32
    )


def layout(n_space, n_rep):
    n_x = 2 if n_space % 2 == 0 else 1
    n_core = 2 if n_rep % 2 == 0 else 1
    return {"z": n_space // n_x, "x": n_x, "y": n_rep // n_core, "core": n_core}


def padded_rows(rows, n_devices):
    unit = 8 * n_devices
    return -(-rows // unit) * unit


def kernel(
    n_space, n_rep, per_piece, piece_rows, grad_scale,
    share_ref, x_hbm, pre_hbm, cot_hbm, cw_hbm, ew_hbm,
    gi_hbm, gc_hbm, ge_hbm,
    x_ref, pre_ref, cot_ref, cw_ref, ew_ref, weighted, hid_send, hid_recv, act_send, act_recv,
    spread, taps_in, grads, grads_next, below, gi_ref, mixed,
    acc, landing, total,
    load_sem, store_sem, hid_sems, act_sems, below_sems, rs_send, rs_recv, ag_send, ag_recv,
):
    s, r = lax.axis_index("space"), lax.axis_index("rep")
    sizes = layout(n_space, n_rep)
    n_x, n_core = sizes["x"], sizes["core"]
    here = {"z": s // n_x, "x": s % n_x, "y": r // n_core, "core": r % n_core}
    half_rows, width, channels = pre_ref.shape
    band = width // n_space
    block = half_rows * band

    def peer(axis, at):
        if axis == "z":
            return (at * n_x + here["x"], r)
        if axis == "x":
            return (here["z"] * n_x + at, r)
        if axis == "y":
            return (s, at * n_core + here["core"])
        return (s, here["y"] * n_core + at)

    pairs = ((cot_hbm, cot_ref), (ew_hbm, ew_ref), (pre_hbm, pre_ref), (x_hbm, x_ref), (cw_hbm, cw_ref))
    loads = [pltpu.make_async_copy(a, b, load_sem.at[k]) for k, (a, b) in enumerate(pairs)]
    load_cot, load_ew, load_pre, load_x, load_cw = loads
    for load in loads:
        load.start()

    barrier = pltpu.get_barrier_semaphore()
    partners = [((s + d) % n_space, r) for d in range(1, n_space)]
    for axis in ("y", "core"):
        partners += [peer(axis, (here[axis] + d) % sizes[axis]) for d in range(1, sizes[axis])]
    for partner in partners:
        pl.semaphore_signal(
            barrier, inc=1, device_id=partner, device_id_type=pl.DeviceIdType.MESH
        )

    load_cot.wait()
    weighted[...] = (cot_ref[...].astype(F32) * share_ref[0]).astype(BF16)
    load_ew.wait()
    hidden = dot(weighted[...], ew_ref[...], 1, 1).astype(BF16)
    for j in range(n_space):
        hid_send[j] = hidden[j * block : (j + 1) * block]
    load_pre.wait()
    for j in range(n_space):
        for i in range(half_rows):
            rows = pre_ref[i, j * band : (j + 1) * band, :].astype(F32)
            act_send[j, i * band : (i + 1) * band, :] = jnp.maximum(rows, 0.0).astype(BF16)
    pl.semaphore_wait(barrier, len(partners))

    def exchange(source, target, sems):
        copies = []
        for d in range(1, n_space):
            to = (s + d) % n_space
            copies.append(
                pltpu.make_async_remote_copy(
                    src_ref=source.at[to],
                    dst_ref=target.at[s],
                    send_sem=sems.at[0, d],
                    recv_sem=sems.at[1, d],
                    device_id=(to, r),
                    device_id_type=pl.DeviceIdType.MESH,
                )
            )
            copies[-1].start()
        target[s] = source[s]
        return copies

    hid_copies = exchange(hid_send, hid_recv, hid_sems)

    out_at = lax.broadcasted_iota(jnp.int32, (2 * width, 2 * width), 0)
    in_at = lax.broadcasted_iota(jnp.int32, (2 * width, 2 * width), 1)
    wanted = jnp.where(in_at < width, 2 * in_at, 2 * (in_at - width) + 1)
    spread[...] = jnp.where(out_at == wanted, 1.0, 0.0).astype(BF16)
    load_x.wait()
    for row in range(2 * half_rows):
        split = dot(x_ref[row], spread[...], 0, 0).astype(BF16)
        at = (row // 2) * width
        for parity in range(2):
            taps_in[row % 2, parity, :, at : at + width] = split[
                :, parity * width : (parity + 1) * width
            ]

    for copy in hid_copies:
        copy.wait()

    column = lax.broadcasted_iota(jnp.int32, (width, channels), 0)

    def put_grad(i, value):
        grads[i * width : (i + 1) * width, :] = value.astype(BF16)
        moved = jnp.where(column < width - 1, pltpu.roll(value, width - 1, 0), 0.0)
        grads_next[i * width : (i + 1) * width, :] = moved.astype(BF16)

    for i in range(half_rows):
        arrived = jnp.concatenate(
            [hid_recv[j, i * band : (i + 1) * band, :].astype(F32) for j in range(n_space)], axis=0
        )
        put_grad(i, jnp.where(pre_ref[i].astype(F32) > 0, arrived, 0.0))
    below_copy = pltpu.make_async_remote_copy(
        src_ref=grads.at[0:width],
        dst_ref=below,
        send_sem=below_sems.at[0],
        recv_sem=below_sems.at[1],
        device_id=((s + n_space - 1) % n_space, r),
        device_id_type=pl.DeviceIdType.MESH,
    )

    @pl.when(s > 0)
    def _():
        below_copy.start()

    act_copies = exchange(act_send, act_recv, act_sems)
    span = half_rows * width
    deep = weighted.shape[1]
    n_units = len(UNITS) + deep // channels
    n_pieces = -(-n_units // per_piece)

    def unit_row(unit):
        return unit // per_piece * piece_rows + unit % per_piece * channels

    def conv_unit(unit):
        row_tap, col_tap = UNITS[unit]
        first = width if row_tap == 0 else 0
        grad = grads_next if col_tap == 0 else grads
        at = unit_row(unit)
        acc[at : at + channels, :] = dot(
            taps_in[(row_tap + 1) % 2, (col_tap + 1) % 2], grad[first : first + span, :], 1, 0
        )

    def expand_units():
        for copy in act_copies:
            copy.wait()
        active = act_recv[...].astype(F32).reshape(n_space * block, channels).astype(BF16)
        for k in range(deep // channels):
            at = unit_row(len(UNITS) + k)
            acc[at : at + channels, :] = dot(
                active, weighted[:, k * channels : (k + 1) * channels], 0, 0
            )

    def low_units():
        @pl.when(s < n_space - 1)
        def _():
            below_copy.wait_recv()

        last = jnp.where(s < n_space - 1, 1.0, 0.0)
        put_grad(half_rows, jnp.where(last > 0.5, below[...].astype(F32), 0.0))
        for unit in range(6, 9):
            conv_unit(unit)

    def piece(k):
        base, length = k * piece_rows, piece_rows
        slot, sem = base, 0
        levels = []
        for axis in ("core",) + tuple(ORDERS[k % len(ORDERS)]):
            n, at = sizes[axis], here[axis]
            if n == 1:
                continue
            sub = length // n
            copies, slots = [], []
            for d in range(1, n):
                to = (at + d) % n
                copies.append(
                    pltpu.make_async_remote_copy(
                        src_ref=acc.at[pl.ds(pl.multiple_of(base + to * sub, 8), sub)],
                        dst_ref=landing.at[pl.ds(slot, sub)],
                        send_sem=rs_send.at[k, sem],
                        recv_sem=rs_recv.at[k, sem],
                        device_id=peer(axis, to),
                        device_id_type=pl.DeviceIdType.MESH,
                    )
                )
                copies[-1].start()
                slots.append(slot)
                slot += sub
                sem += 1
            yield axis, sub
            for copy in copies:
                copy.wait()
            base = base + at * sub
            own = pl.ds(pl.multiple_of(base, 8), sub)
            value = acc[own, :]
            for place in slots:
                value = value + landing[place : place + sub, :]
            acc[own, :] = value
            length = sub
            levels.append((axis, n, at, base, sub))
        total[own, :] = value * grad_scale
        sem = 0
        for axis, n, at, base, sub in reversed(levels):
            copies = []
            mine = total.at[pl.ds(pl.multiple_of(base, 8), sub)]
            for d in range(1, n):
                copies.append(
                    pltpu.make_async_remote_copy(
                        src_ref=mine,
                        dst_ref=mine,
                        send_sem=ag_send.at[k, sem],
                        recv_sem=ag_recv.at[k, sem],
                        device_id=peer(axis, (at + d) % n),
                        device_id_type=pl.DeviceIdType.MESH,
                    )
                )
                copies[-1].start()
                sem += 1
            yield axis, sub
            for copy in copies:
                copy.wait()
        for unit in range(k * per_piece, min((k + 1) * per_piece, n_units)):
            rows = total.at[pl.ds(unit_row(unit), channels)]
            if unit < len(UNITS):
                p, q = UNITS[unit]
                target = gc_hbm.at[p, pl.ds(q * channels, channels)]
            else:
                target = ge_hbm.at[:, pl.ds((unit - len(UNITS)) * channels, channels)]
            stores.append(
                pltpu.make_async_copy(rows, target, store_sem.at[2 * half_rows + unit])
            )
            stores[-1].start()

    def term(first, row_tap, col_tap):
        grad = grads_next if col_tap == 0 else grads
        return dot(grad[first : first + span, :], cw_ref[row_tap, col_tap], 1, 1)

    def input_parts():
        load_cw.wait()
        for row_parity in range(2):
            pairs = [(0, 1)] if row_parity == 0 else [(0, 2), (width, 0)]
            for parity in range(2):
                cols = (1,) if parity == 0 else (2, 0)
                terms = [term(first, p, q) for first, p in pairs for q in cols]
                mixed[parity] = functools.reduce(jnp.add, terms).astype(BF16)
                yield
            for i in range(half_rows):
                both = jnp.concatenate(
                    [mixed[parity, i * width : (i + 1) * width, :] for parity in range(2)], axis=0
                )
                row = 2 * i + row_parity
                gi_ref[row] = dot(spread[...], both, 1, 0).astype(BF16)
                stores.append(
                    pltpu.make_async_copy(gi_ref.at[row], gi_hbm.at[row], store_sem.at[row])
                )
                stores[-1].start()
                yield

    stores = []
    pieces = [piece(k) for k in range(n_pieces)]
    filler = input_parts()
    line_free = dict.fromkeys(sizes, 0.0)
    line_cost = {"core": 1 / 6, "x": 2.0, "y": 2.0, "z": 2.0 * (sizes["z"] // 2) ** 2}
    per_row = channels * 4e-5
    done_units = set()
    begun = set()
    events = []
    clock = 0.0

    def advance(k):
        stage = next(pieces[k], None)
        if stage is not None:
            axis, sub = stage
            begin = max(clock, line_free[axis])
            line_free[axis] = begin + sub * per_row * line_cost[axis]
            heapq.heappush(events, (line_free[axis] + 1.5, 2, k))

    def ready(units):
        done_units.update(units)
        for k in range(n_pieces):
            members = range(k * per_piece, min((k + 1) * per_piece, n_units))
            if k not in begun and done_units.issuperset(members):
                begun.add(k)
                used = len(members) * channels
                if used < piece_rows:
                    acc[k * piece_rows + used : (k + 1) * piece_rows, :] = jnp.zeros(
                        (piece_rows - used, channels), F32
                    )
                advance(k)

    heapq.heappush(events, (4.0, 0, 0))
    heapq.heappush(events, (7.0, 1, 0))
    for unit in range(6):
        conv_unit(unit)
        ready([unit])
        clock += 0.2
    low_done = False
    while events:
        while low_done and events[0][0] > clock + 0.3 and next(filler, "end") != "end":
            clock += 0.4
        when, kind, k = heapq.heappop(events)
        clock = max(clock, when)
        if kind == 0:
            low_units()
            low_done = True
            ready([6, 7, 8])
            clock += 0.6
        elif kind == 1:
            expand_units()
            ready(range(len(UNITS), n_units))
            clock += 0.8
        else:
            advance(k)
            clock += 0.1
    for _ in filler:
        pass

    @pl.when(s > 0)
    def _():
        below_copy.wait_send()

    for store in stores:
        store.wait()


def body(n_space, n_rep, stem_input, stem_preact, deep_cotangent, tissue_tiles, conv_weight, expand_weight):
    share = tissue_tiles.astype(F32) / TILES
    _, in_rows, cols, channels = stem_input.shape
    _, half_rows, width, _ = stem_preact.shape
    _, deep_rows, band, deep = deep_cotangent.shape
    devices = n_space * n_rep
    block = half_rows * band
    per_piece = -(-8 * devices // channels)
    piece_rows = padded_rows(per_piece * channels, devices)
    n_units = len(UNITS) + deep // channels
    n_pieces = -(-n_units // per_piece)
    all_rows = n_pieces * piece_rows
    grad_scale = float(n_rep * half_rows * n_space * width) ** (-0.5)
    sizes = layout(n_space, n_rep)
    copies = sum(n - 1 for n in sizes.values())
    anywhere = pl.BlockSpec(memory_space=pl.ANY)
    dma = pltpu.SemaphoreType.DMA
    grad_input, conv_sum, expand_sum = pl.pallas_call(
        functools.partial(kernel, n_space, n_rep, per_piece, piece_rows, grad_scale),
        out_shape=(
            jax.ShapeDtypeStruct((in_rows, cols, channels), BF16),
            jax.ShapeDtypeStruct((3, 3 * channels, channels), F32),
            jax.ShapeDtypeStruct((channels, deep), F32),
        ),
        in_specs=[
            pl.BlockSpec(memory_space=pltpu.SMEM),
            *[pl.BlockSpec(memory_space=pltpu.HBM)] * 5,
        ],
        out_specs=(anywhere, anywhere, anywhere),
        scratch_shapes=[
            pltpu.VMEM((in_rows, cols, channels), BF16),
            pltpu.VMEM(stem_preact.shape[1:], BF16),
            pltpu.VMEM((deep_rows * band, deep), BF16),
            pltpu.VMEM(conv_weight.shape, BF16),
            pltpu.VMEM(expand_weight.shape, BF16),
            pltpu.VMEM((deep_rows * band, deep), BF16),
            pltpu.VMEM((n_space, block, channels), BF16),
            pltpu.VMEM((n_space, block, channels), BF16),
            pltpu.VMEM((n_space, block, channels), BF16),
            pltpu.VMEM((n_space, block, channels), BF16),
            pltpu.VMEM((cols, cols), BF16),
            pltpu.VMEM((2, 2, channels, half_rows * width), BF16),
            pltpu.VMEM(((half_rows + 1) * width, channels), BF16),
            pltpu.VMEM(((half_rows + 1) * width, channels), BF16),
            pltpu.VMEM((width, channels), BF16),
            pltpu.VMEM((in_rows, cols, channels), BF16),
            pltpu.VMEM((2, half_rows * width, channels), BF16),
            pltpu.VMEM((all_rows, channels), F32),
            pltpu.VMEM((all_rows, channels), F32),
            pltpu.VMEM((all_rows, channels), F32),
            dma((5,)),
            dma((in_rows + n_units,)),
            dma((2, n_space)),
            dma((2, n_space)),
            dma((2,)),
            dma((n_pieces, copies)),
            dma((n_pieces, copies)),
            dma((n_pieces, copies)),
            dma((n_pieces, copies)),
        ],
        compiler_params=pltpu.CompilerParams(
            collective_id=0, has_side_effects=True, vmem_limit_bytes=VMEM_LIMIT
        ),
    )(
        share,
        stem_input[0],
        stem_preact[0],
        deep_cotangent.reshape(deep_rows * band, deep),
        conv_weight,
        expand_weight,
    )
    return (grad_input[None], conv_sum.reshape(3, 3, channels, channels), expand_sum)


def solution(mesh):
    return jax.shard_map(
        functools.partial(body, mesh.shape["space"], mesh.shape["rep"]),
        mesh=mesh,
        in_specs=(
            P("rep", "space", None, None),
            P("rep", "space", None, None),
            P("rep", None, "space", None),
            P("rep"),
            P(),
            P(),
        ),
        out_specs=(P("rep", "space", None, None), P(), P()),
        check_vma=False,
    )
```

```python
import functools
import heapq

import jax
import jax.numpy as jnp
from jax import lax
from jax.experimental import pallas as pl
from jax.experimental.pallas import tpu as pltpu
from jax.sharding import PartitionSpec as P

TILES = 64
VMEM_LIMIT = 56 * 1024 * 1024
F32, BF16 = jnp.float32, jnp.bfloat16
ORDERS = ("xyz", "yxz", "xzy", "yxz", "xyz", "yzx")
UNITS = tuple((p, q) for p in (1, 2, 0) for q in range(3))


def dot(lhs, rhs, lhs_dim, rhs_dim):
    return lax.dot_general(
        lhs, rhs, (((lhs_dim,), (rhs_dim,)), ((), ())), preferred_element_type=F32
    )


def layout(n_space, n_rep):
    n_x = 2 if n_space % 2 == 0 else 1
    n_core = 2 if n_rep % 2 == 0 else 1
    return {"z": n_space // n_x, "x": n_x, "y": n_rep // n_core, "core": n_core}


def padded_rows(rows, n_devices):
    unit = 8 * n_devices
    return -(-rows // unit) * unit


def kernel(
    n_space, n_rep, per_piece, piece_rows, grad_scale,
    share_ref, x_hbm, pre_hbm, cot_hbm, cw_hbm, ew_hbm,
    gi_hbm, gc_hbm, ge_hbm,
    x_ref, pre_ref, cot_ref, cw_ref, ew_ref, weighted, hid_send, hid_recv, act_send, act_recv,
    spread, taps_in, grads, grads_next, below, gi_ref, mixed,
    acc, landing, total,
    load_sem, store_sem, hid_sems, act_sems, below_sems, rs_send, rs_recv, ag_send, ag_recv,
):
    s, r = lax.axis_index("space"), lax.axis_index("rep")
    sizes = layout(n_space, n_rep)
    n_x, n_core = sizes["x"], sizes["core"]
    here = {"z": s // n_x, "x": s % n_x, "y": r // n_core, "core": r % n_core}
    half_rows, width, channels = pre_ref.shape
    band = width // n_space
    block = half_rows * band

    def peer(axis, at):
        if axis == "z":
            return (at * n_x + here["x"], r)
        if axis == "x":
            return (here["z"] * n_x + at, r)
        if axis == "y":
            return (s, at * n_core + here["core"])
        return (s, here["y"] * n_core + at)

    pairs = ((pre_hbm, pre_ref), (cot_hbm, cot_ref), (ew_hbm, ew_ref), (x_hbm, x_ref), (cw_hbm, cw_ref))
    loads = [pltpu.make_async_copy(a, b, load_sem.at[k]) for k, (a, b) in enumerate(pairs)]
    load_pre, load_cot, load_ew, load_x, load_cw = loads
    for load in loads:
        load.start()

    barrier = pltpu.get_barrier_semaphore()
    partners = [((s + d) % n_space, r) for d in range(1, n_space)]
    for axis in ("y", "core"):
        partners += [peer(axis, (here[axis] + d) % sizes[axis]) for d in range(1, sizes[axis])]
    for partner in partners:
        pl.semaphore_signal(
            barrier, inc=1, device_id=partner, device_id_type=pl.DeviceIdType.MESH
        )

    load_pre.wait()
    for j in range(n_space):
        for i in range(half_rows):
            rows = pre_ref[i, j * band : (j + 1) * band, :].astype(F32)
            act_send[j, i * band : (i + 1) * band, :] = jnp.maximum(rows, 0.0).astype(BF16)
    load_cot.wait()
    weighted[...] = (cot_ref[...].astype(F32) * share_ref[0]).astype(BF16)
    load_ew.wait()
    pl.semaphore_wait(barrier, len(partners))

    def exchange(source, target, sems):
        copies = []
        for d in range(1, n_space):
            to = (s + d) % n_space
            copies.append(
                pltpu.make_async_remote_copy(
                    src_ref=source.at[to],
                    dst_ref=target.at[s],
                    send_sem=sems.at[0, d],
                    recv_sem=sems.at[1, d],
                    device_id=(to, r),
                    device_id_type=pl.DeviceIdType.MESH,
                )
            )
            copies[-1].start()
        target[s] = source[s]
        return copies

    act_copies = exchange(act_send, act_recv, act_sems)
    hidden = dot(weighted[...], ew_ref[...], 1, 1).astype(BF16)
    for j in range(n_space):
        hid_send[j] = hidden[j * block : (j + 1) * block]
    hid_copies = exchange(hid_send, hid_recv, hid_sems)

    out_at = lax.broadcasted_iota(jnp.int32, (2 * width, 2 * width), 0)
    in_at = lax.broadcasted_iota(jnp.int32, (2 * width, 2 * width), 1)
    wanted = jnp.where(in_at < width, 2 * in_at, 2 * (in_at - width) + 1)
    spread[...] = jnp.where(out_at == wanted, 1.0, 0.0).astype(BF16)
    load_x.wait()
    for row in range(2 * half_rows):
        split = dot(x_ref[row], spread[...], 0, 0).astype(BF16)
        at = (row // 2) * width
        for parity in range(2):
            taps_in[row % 2, parity, :, at : at + width] = split[
                :, parity * width : (parity + 1) * width
            ]

    span = half_rows * width
    deep = weighted.shape[1]
    n_units = len(UNITS) + deep // channels
    n_pieces = -(-n_units // per_piece)

    def unit_row(unit):
        return unit // per_piece * piece_rows + unit % per_piece * channels

    def conv_unit(unit):
        row_tap, col_tap = UNITS[unit]
        first = width if row_tap == 0 else 0
        grad = grads_next if col_tap == 0 else grads
        at = unit_row(unit)
        acc[at : at + channels, :] = dot(
            taps_in[(row_tap + 1) % 2, (col_tap + 1) % 2], grad[first : first + span, :], 1, 0
        )

    def expand_units():
        for copy in act_copies:
            copy.wait()
        active = act_recv[...].astype(F32).reshape(n_space * block, channels).astype(BF16)
        for k in range(deep // channels):
            at = unit_row(len(UNITS) + k)
            acc[at : at + channels, :] = dot(
                active, weighted[:, k * channels : (k + 1) * channels], 0, 0
            )

    def low_units():
        @pl.when(s < n_space - 1)
        def _():
            below_copy.wait_recv()

        last = jnp.where(s < n_space - 1, 1.0, 0.0)
        put_grad(half_rows, jnp.where(last > 0.5, below[...].astype(F32), 0.0))
        for unit in range(6, 9):
            conv_unit(unit)

    def piece(k):
        base, length = k * piece_rows, piece_rows
        slot, sem = base, 0
        levels = []
        for axis in ("core",) + tuple(ORDERS[k % len(ORDERS)]):
            n, at = sizes[axis], here[axis]
            if n == 1:
                continue
            sub = length // n
            copies, slots = [], []
            for d in range(1, n):
                to = (at + d) % n
                copies.append(
                    pltpu.make_async_remote_copy(
                        src_ref=acc.at[pl.ds(pl.multiple_of(base + to * sub, 8), sub)],
                        dst_ref=landing.at[pl.ds(slot, sub)],
                        send_sem=rs_send.at[k, sem],
                        recv_sem=rs_recv.at[k, sem],
                        device_id=peer(axis, to),
                        device_id_type=pl.DeviceIdType.MESH,
                    )
                )
                copies[-1].start()
                slots.append(slot)
                slot += sub
                sem += 1
            yield axis, sub
            for copy in copies:
                copy.wait()
            base = base + at * sub
            own = pl.ds(pl.multiple_of(base, 8), sub)
            value = acc[own, :]
            for place in slots:
                value = value + landing[place : place + sub, :]
            acc[own, :] = value
            length = sub
            levels.append((axis, n, at, base, sub))
        total[own, :] = value * grad_scale
        sem = 0
        for axis, n, at, base, sub in reversed(levels):
            copies = []
            mine = total.at[pl.ds(pl.multiple_of(base, 8), sub)]
            for d in range(1, n):
                copies.append(
                    pltpu.make_async_remote_copy(
                        src_ref=mine,
                        dst_ref=mine,
                        send_sem=ag_send.at[k, sem],
                        recv_sem=ag_recv.at[k, sem],
                        device_id=peer(axis, (at + d) % n),
                        device_id_type=pl.DeviceIdType.MESH,
                    )
                )
                copies[-1].start()
                sem += 1
            yield axis, sub
            for copy in copies:
                copy.wait()
        for unit in range(k * per_piece, min((k + 1) * per_piece, n_units)):
            rows = total.at[pl.ds(unit_row(unit), channels)]
            if unit < len(UNITS):
                p, q = UNITS[unit]
                target = gc_hbm.at[p, pl.ds(q * channels, channels)]
            else:
                target = ge_hbm.at[:, pl.ds((unit - len(UNITS)) * channels, channels)]
            stores.append(
                pltpu.make_async_copy(rows, target, store_sem.at[2 * half_rows + unit])
            )
            stores[-1].start()

    def term(first, row_tap, col_tap):
        grad = grads_next if col_tap == 0 else grads
        return dot(grad[first : first + span, :], cw_ref[row_tap, col_tap], 1, 1)

    def input_parts():
        load_cw.wait()
        for row_parity in range(2):
            pairs = [(0, 1)] if row_parity == 0 else [(0, 2), (width, 0)]
            for parity in range(2):
                cols = (1,) if parity == 0 else (2, 0)
                terms = [term(first, p, q) for first, p in pairs for q in cols]
                mixed[parity] = functools.reduce(jnp.add, terms).astype(BF16)
                yield
            for i in range(half_rows):
                both = jnp.concatenate(
                    [mixed[parity, i * width : (i + 1) * width, :] for parity in range(2)], axis=0
                )
                row = 2 * i + row_parity
                gi_ref[row] = dot(spread[...], both, 1, 0).astype(BF16)
                stores.append(
                    pltpu.make_async_copy(gi_ref.at[row], gi_hbm.at[row], store_sem.at[row])
                )
                stores[-1].start()
                yield

    stores = []
    pieces = [piece(k) for k in range(n_pieces)]
    filler = input_parts()
    line_free = dict.fromkeys(sizes, 0.0)
    line_cost = {"core": 1 / 6, "x": 2.0, "y": 2.0, "z": 2.0 * (sizes["z"] // 2) ** 2}
    per_row = channels * 4e-5
    done_units = set()
    begun = set()
    events = []
    clock = 0.0

    def advance(k):
        stage = next(pieces[k], None)
        if stage is not None:
            axis, sub = stage
            begin = max(clock, line_free[axis])
            line_free[axis] = begin + sub * per_row * line_cost[axis]
            heapq.heappush(events, (line_free[axis] + 1.5, 2, k))

    def ready(units):
        done_units.update(units)
        for k in range(n_pieces):
            members = range(k * per_piece, min((k + 1) * per_piece, n_units))
            if k not in begun and done_units.issuperset(members):
                begun.add(k)
                used = len(members) * channels
                if used < piece_rows:
                    acc[k * piece_rows + used : (k + 1) * piece_rows, :] = jnp.zeros(
                        (piece_rows - used, channels), F32
                    )
                advance(k)

    column = lax.broadcasted_iota(jnp.int32, (width, channels), 0)

    def put_grad(i, value):
        grads[i * width : (i + 1) * width, :] = value.astype(BF16)
        moved = jnp.where(column < width - 1, pltpu.roll(value, width - 1, 0), 0.0)
        grads_next[i * width : (i + 1) * width, :] = moved.astype(BF16)

    expand_units()
    ready(range(len(UNITS), n_units))
    while events and events[0][0] < 3.0:
        clock, _, k = heapq.heappop(events)
        advance(k)
    for copy in hid_copies:
        copy.wait()

    for i in range(half_rows):
        arrived = jnp.concatenate(
            [hid_recv[j, i * band : (i + 1) * band, :].astype(F32) for j in range(n_space)], axis=0
        )
        put_grad(i, jnp.where(pre_ref[i].astype(F32) > 0, arrived, 0.0))
    below_copy = pltpu.make_async_remote_copy(
        src_ref=grads.at[0:width],
        dst_ref=below,
        send_sem=below_sems.at[0],
        recv_sem=below_sems.at[1],
        device_id=((s + n_space - 1) % n_space, r),
        device_id_type=pl.DeviceIdType.MESH,
    )

    @pl.when(s > 0)
    def _():
        below_copy.start()

    clock = 4.0
    for unit in range(6):
        conv_unit(unit)
        ready([unit])
        clock += 0.2
        while events and events[0][0] < clock:
            advance(heapq.heappop(events)[2])
    heapq.heappush(events, (8.0, 0, 0))
    low_done = False
    while events:
        while low_done and events[0][0] > clock + 0.3 and next(filler, "end") != "end":
            clock += 0.4
        when, kind, k = heapq.heappop(events)
        clock = max(clock, when)
        if kind == 0:
            low_units()
            low_done = True
            ready([6, 7, 8])
            clock += 0.6
        else:
            advance(k)
            clock += 0.1
    for _ in filler:
        pass

    @pl.when(s > 0)
    def _():
        below_copy.wait_send()

    for store in stores:
        store.wait()


def body(n_space, n_rep, stem_input, stem_preact, deep_cotangent, tissue_tiles, conv_weight, expand_weight):
    share = tissue_tiles.astype(F32) / TILES
    _, in_rows, cols, channels = stem_input.shape
    _, half_rows, width, _ = stem_preact.shape
    _, deep_rows, band, deep = deep_cotangent.shape
    devices = n_space * n_rep
    block = half_rows * band
    per_piece = -(-8 * devices // channels)
    piece_rows = padded_rows(per_piece * channels, devices)
    n_units = len(UNITS) + deep // channels
    n_pieces = -(-n_units // per_piece)
    all_rows = n_pieces * piece_rows
    grad_scale = float(n_rep * half_rows * n_space * width) ** (-0.5)
    sizes = layout(n_space, n_rep)
    copies = sum(n - 1 for n in sizes.values())
    anywhere = pl.BlockSpec(memory_space=pl.ANY)
    dma = pltpu.SemaphoreType.DMA
    grad_input, conv_sum, expand_sum = pl.pallas_call(
        functools.partial(kernel, n_space, n_rep, per_piece, piece_rows, grad_scale),
        out_shape=(
            jax.ShapeDtypeStruct((in_rows, cols, channels), BF16),
            jax.ShapeDtypeStruct((3, 3 * channels, channels), F32),
            jax.ShapeDtypeStruct((channels, deep), F32),
        ),
        in_specs=[
            pl.BlockSpec(memory_space=pltpu.SMEM),
            *[pl.BlockSpec(memory_space=pltpu.HBM)] * 5,
        ],
        out_specs=(anywhere, anywhere, anywhere),
        scratch_shapes=[
            pltpu.VMEM((in_rows, cols, channels), BF16),
            pltpu.VMEM(stem_preact.shape[1:], BF16),
            pltpu.VMEM((deep_rows * band, deep), BF16),
            pltpu.VMEM(conv_weight.shape, BF16),
            pltpu.VMEM(expand_weight.shape, BF16),
            pltpu.VMEM((deep_rows * band, deep), BF16),
            pltpu.VMEM((n_space, block, channels), BF16),
            pltpu.VMEM((n_space, block, channels), BF16),
            pltpu.VMEM((n_space, block, channels), BF16),
            pltpu.VMEM((n_space, block, channels), BF16),
            pltpu.VMEM((cols, cols), BF16),
            pltpu.VMEM((2, 2, channels, half_rows * width), BF16),
            pltpu.VMEM(((half_rows + 1) * width, channels), BF16),
            pltpu.VMEM(((half_rows + 1) * width, channels), BF16),
            pltpu.VMEM((width, channels), BF16),
            pltpu.VMEM((in_rows, cols, channels), BF16),
            pltpu.VMEM((2, half_rows * width, channels), BF16),
            pltpu.VMEM((all_rows, channels), F32),
            pltpu.VMEM((all_rows, channels), F32),
            pltpu.VMEM((all_rows, channels), F32),
            dma((5,)),
            dma((in_rows + n_units,)),
            dma((2, n_space)),
            dma((2, n_space)),
            dma((2,)),
            dma((n_pieces, copies)),
            dma((n_pieces, copies)),
            dma((n_pieces, copies)),
            dma((n_pieces, copies)),
        ],
        compiler_params=pltpu.CompilerParams(
            collective_id=0, has_side_effects=True, vmem_limit_bytes=VMEM_LIMIT
        ),
    )(
        share,
        stem_input[0],
        stem_preact[0],
        deep_cotangent.reshape(deep_rows * band, deep),
        conv_weight,
        expand_weight,
    )
    return (grad_input[None], conv_sum.reshape(3, 3, channels, channels), expand_sum)


def solution(mesh):
    return jax.shard_map(
        functools.partial(body, mesh.shape["space"], mesh.shape["rep"]),
        mesh=mesh,
        in_specs=(
            P("rep", "space", None, None),
            P("rep", "space", None, None),
            P("rep", None, "space", None),
            P("rep"),
            P(),
            P(),
        ),
        out_specs=(P("rep", "space", None, None), P(), P()),
        check_vma=False,
    )
```

```python
import functools
import heapq

import jax
import jax.numpy as jnp
from jax import lax
from jax.experimental import pallas as pl
from jax.experimental.pallas import tpu as pltpu
from jax.sharding import PartitionSpec as P

TILES = 64
VMEM_LIMIT = 32 * 1024 * 1024
F32, BF16 = jnp.float32, jnp.bfloat16
ORDERS = ("xyz", "yxz", "xzy", "yzx", "xyz", "yxz", "xyz")
UNITS = tuple((p, q) for p in (1, 2, 0) for q in range(3))


def dot(lhs, rhs, lhs_dim, rhs_dim):
    return lax.dot_general(
        lhs, rhs, (((lhs_dim,), (rhs_dim,)), ((), ())), preferred_element_type=F32
    )


def layout(n_space, n_rep):
    n_x = 2 if n_space % 2 == 0 else 1
    n_core = 2 if n_rep % 2 == 0 else 1
    return {"z": n_space // n_x, "x": n_x, "y": n_rep // n_core, "core": n_core}


def padded_rows(rows, n_devices):
    unit = 8 * n_devices
    return -(-rows // unit) * unit


def kernel(
    n_space, n_rep, per_piece, piece_rows, grad_scale,
    share_ref, x_hbm, pre_hbm, cot_hbm, cw_hbm, ew_hbm,
    gi_hbm, gc_hbm, ge_hbm,
    x_ref, pre_ref, cot_ref, cw_ref, ew_ref, weighted, hid_send, hid_recv, act_send, act_recv,
    spread, taps_in, grads, grads_next, below, gi_ref, mixed,
    acc, landing, total,
    load_sem, store_sem, hid_sems, act_sems, below_sems, rs_send, rs_recv, ag_send, ag_recv,
):
    s, r = lax.axis_index("space"), lax.axis_index("rep")
    sizes = layout(n_space, n_rep)
    n_x, n_core = sizes["x"], sizes["core"]
    here = {"z": s // n_x, "x": s % n_x, "y": r // n_core, "core": r % n_core}
    half_rows, width, channels = pre_ref.shape
    band = width // n_space
    block = half_rows * band

    def peer(axis, at):
        if axis == "z":
            return (at * n_x + here["x"], r)
        if axis == "x":
            return (here["z"] * n_x + at, r)
        if axis == "y":
            return (s, at * n_core + here["core"])
        return (s, here["y"] * n_core + at)

    pairs = ((cot_hbm, cot_ref), (ew_hbm, ew_ref), (pre_hbm, pre_ref), (x_hbm, x_ref), (cw_hbm, cw_ref))
    loads = [pltpu.make_async_copy(a, b, load_sem.at[k]) for k, (a, b) in enumerate(pairs)]
    load_cot, load_ew, load_pre, load_x, load_cw = loads
    for load in loads:
        load.start()

    barrier = pltpu.get_barrier_semaphore()
    partners = [((s + d) % n_space, r) for d in range(1, n_space)]
    for axis in ("y", "core"):
        partners += [peer(axis, (here[axis] + d) % sizes[axis]) for d in range(1, sizes[axis])]
    for partner in partners:
        pl.semaphore_signal(
            barrier, inc=1, device_id=partner, device_id_type=pl.DeviceIdType.MESH
        )

    load_cot.wait()
    weighted[...] = (cot_ref[...].astype(F32) * share_ref[0]).astype(BF16)
    load_ew.wait()
    hidden = dot(weighted[...], ew_ref[...], 1, 1).astype(BF16)
    for j in range(n_space):
        hid_send[j] = hidden[j * block : (j + 1) * block]
    load_pre.wait()
    for j in range(n_space):
        for i in range(half_rows):
            rows = pre_ref[i, j * band : (j + 1) * band, :].astype(F32)
            act_send[j, i * band : (i + 1) * band, :] = jnp.maximum(rows, 0.0).astype(BF16)
    pl.semaphore_wait(barrier, len(partners))

    def exchange(source, target, sems):
        copies = []
        for d in range(1, n_space):
            to = (s + d) % n_space
            copies.append(
                pltpu.make_async_remote_copy(
                    src_ref=source.at[to],
                    dst_ref=target.at[s],
                    send_sem=sems.at[0, d],
                    recv_sem=sems.at[1, d],
                    device_id=(to, r),
                    device_id_type=pl.DeviceIdType.MESH,
                )
            )
            copies[-1].start()
        target[s] = source[s]
        return copies

    hid_copies = exchange(hid_send, hid_recv, hid_sems)

    out_at = lax.broadcasted_iota(jnp.int32, (2 * width, 2 * width), 0)
    in_at = lax.broadcasted_iota(jnp.int32, (2 * width, 2 * width), 1)
    wanted = jnp.where(in_at < width, 2 * in_at, 2 * (in_at - width) + 1)
    spread[...] = jnp.where(out_at == wanted, 1.0, 0.0).astype(BF16)
    load_x.wait()
    for row in range(2 * half_rows):
        split = dot(x_ref[row], spread[...], 0, 0).astype(BF16)
        at = (row // 2) * width
        for parity in range(2):
            taps_in[row % 2, parity, :, at : at + width] = split[
                :, parity * width : (parity + 1) * width
            ]

    for copy in hid_copies:
        copy.wait()

    column = lax.broadcasted_iota(jnp.int32, (width, channels), 0)

    def put_grad(i, value):
        grads[i * width : (i + 1) * width, :] = value.astype(BF16)
        moved = jnp.where(column < width - 1, pltpu.roll(value, width - 1, 0), 0.0)
        grads_next[i * width : (i + 1) * width, :] = moved.astype(BF16)

    for i in range(half_rows):
        arrived = jnp.concatenate(
            [hid_recv[j, i * band : (i + 1) * band, :].astype(F32) for j in range(n_space)], axis=0
        )
        put_grad(i, jnp.where(pre_ref[i].astype(F32) > 0, arrived, 0.0))
    below_copy = pltpu.make_async_remote_copy(
        src_ref=grads.at[0:width],
        dst_ref=below,
        send_sem=below_sems.at[0],
        recv_sem=below_sems.at[1],
        device_id=((s + n_space - 1) % n_space, r),
        device_id_type=pl.DeviceIdType.MESH,
    )

    @pl.when(s > 0)
    def _():
        below_copy.start()

    act_copies = exchange(act_send, act_recv, act_sems)
    span = half_rows * width
    deep = weighted.shape[1]
    n_units = len(UNITS) + deep // channels
    n_pieces = -(-n_units // per_piece)

    def unit_row(unit):
        return unit // per_piece * piece_rows + unit % per_piece * channels

    def piece_length(k):
        members = min((k + 1) * per_piece, n_units) - k * per_piece
        return padded_rows(members * channels, n_space * n_rep)

    def conv_unit(unit):
        row_tap, col_tap = UNITS[unit]
        first = width if row_tap == 0 else 0
        grad = grads_next if col_tap == 0 else grads
        at = unit_row(unit)
        acc[at : at + channels, :] = dot(
            taps_in[(row_tap + 1) % 2, (col_tap + 1) % 2], grad[first : first + span, :], 1, 0
        )

    def expand_units():
        for copy in act_copies:
            copy.wait()
        active = act_recv[...].astype(F32).reshape(n_space * block, channels).astype(BF16)
        for k in range(deep // channels):
            at = unit_row(len(UNITS) + k)
            acc[at : at + channels, :] = dot(
                active, weighted[:, k * channels : (k + 1) * channels], 0, 0
            )

    def low_units():
        @pl.when(s < n_space - 1)
        def _():
            below_copy.wait_recv()

        last = jnp.where(s < n_space - 1, 1.0, 0.0)
        put_grad(half_rows, jnp.where(last > 0.5, below[...].astype(F32), 0.0))
        for unit in range(6, 9):
            conv_unit(unit)

    def piece(k):
        base, length = k * piece_rows, piece_length(k)
        slot, sem = base, 0
        levels = []
        for axis in ("core",) + tuple(ORDERS[k % len(ORDERS)]):
            n, at = sizes[axis], here[axis]
            if n == 1:
                continue
            sub = length // n
            copies, slots = [], []
            for d in range(1, n):
                to = (at + d) % n
                copies.append(
                    pltpu.make_async_remote_copy(
                        src_ref=acc.at[pl.ds(pl.multiple_of(base + to * sub, 8), sub)],
                        dst_ref=landing.at[pl.ds(slot, sub)],
                        send_sem=rs_send.at[k, sem],
                        recv_sem=rs_recv.at[k, sem],
                        device_id=peer(axis, to),
                        device_id_type=pl.DeviceIdType.MESH,
                    )
                )
                copies[-1].start()
                slots.append(slot)
                slot += sub
                sem += 1
            yield axis, sub
            for copy in copies:
                copy.wait()
            base = base + at * sub
            own = pl.ds(pl.multiple_of(base, 8), sub)
            value = acc[own, :]
            for place in slots:
                value = value + landing[place : place + sub, :]
            acc[own, :] = value
            length = sub
            levels.append((axis, n, at, base, sub))
        total[own, :] = value * grad_scale
        sem = 0
        for axis, n, at, base, sub in reversed(levels):
            copies = []
            mine = total.at[pl.ds(pl.multiple_of(base, 8), sub)]
            for d in range(1, n):
                copies.append(
                    pltpu.make_async_remote_copy(
                        src_ref=mine,
                        dst_ref=mine,
                        send_sem=ag_send.at[k, sem],
                        recv_sem=ag_recv.at[k, sem],
                        device_id=peer(axis, (at + d) % n),
                        device_id_type=pl.DeviceIdType.MESH,
                    )
                )
                copies[-1].start()
                sem += 1
            yield axis, sub
            for copy in copies:
                copy.wait()
        for unit in range(k * per_piece, min((k + 1) * per_piece, n_units)):
            rows = total.at[pl.ds(unit_row(unit), channels)]
            if unit < len(UNITS):
                p, q = UNITS[unit]
                target = gc_hbm.at[p, pl.ds(q * channels, channels)]
            else:
                target = ge_hbm.at[:, pl.ds((unit - len(UNITS)) * channels, channels)]
            stores.append(
                pltpu.make_async_copy(rows, target, store_sem.at[2 * half_rows + unit])
            )
            stores[-1].start()

    def term(first, row_tap, col_tap):
        grad = grads_next if col_tap == 0 else grads
        return dot(grad[first : first + span, :], cw_ref[row_tap, col_tap], 1, 1)

    def input_parts():
        load_cw.wait()
        for row_parity in range(2):
            pairs = [(0, 1)] if row_parity == 0 else [(0, 2), (width, 0)]
            for parity in range(2):
                cols = (1,) if parity == 0 else (2, 0)
                terms = [term(first, p, q) for first, p in pairs for q in cols]
                mixed[parity] = functools.reduce(jnp.add, terms).astype(BF16)
                yield
            for i in range(half_rows):
                both = jnp.concatenate(
                    [mixed[parity, i * width : (i + 1) * width, :] for parity in range(2)], axis=0
                )
                row = 2 * i + row_parity
                gi_ref[row] = dot(spread[...], both, 1, 0).astype(BF16)
                stores.append(
                    pltpu.make_async_copy(gi_ref.at[row], gi_hbm.at[row], store_sem.at[row])
                )
                stores[-1].start()
                yield

    stores = []
    pieces = [piece(k) for k in range(n_pieces)]
    filler = input_parts()
    line_free = dict.fromkeys(sizes, 0.0)
    line_cost = {"core": 1 / 6, "x": 2.0, "y": 2.0, "z": 2.0 * (sizes["z"] // 2) ** 2}
    per_row = channels * 4e-5
    done_units = set()
    begun = set()
    events = []
    clock = 0.0

    def advance(k):
        stage = next(pieces[k], None)
        if stage is not None:
            axis, sub = stage
            begin = max(clock, line_free[axis])
            line_free[axis] = begin + sub * per_row * line_cost[axis]
            heapq.heappush(events, (line_free[axis] + 1.5, 2, k))

    def ready(units):
        done_units.update(units)
        for k in range(n_pieces):
            members = range(k * per_piece, min((k + 1) * per_piece, n_units))
            if k not in begun and done_units.issuperset(members):
                begun.add(k)
                used = len(members) * channels
                if used < piece_length(k):
                    acc[k * piece_rows + used : k * piece_rows + piece_length(k), :] = jnp.zeros(
                        (piece_length(k) - used, channels), F32
                    )
                advance(k)

    heapq.heappush(events, (4.0, 0, 0))
    heapq.heappush(events, (7.0, 1, 0))
    for unit in range(6):
        conv_unit(unit)
        ready([unit])
        clock += 0.2
    low_done = False
    while events:
        while low_done and events[0][0] > clock + 0.3 and next(filler, "end") != "end":
            clock += 0.4
        when, kind, k = heapq.heappop(events)
        clock = max(clock, when)
        if kind == 0:
            low_units()
            low_done = True
            ready([6, 7, 8])
            clock += 0.6
        elif kind == 1:
            expand_units()
            ready(range(len(UNITS), n_units))
            clock += 0.8
        else:
            advance(k)
            clock += 0.1
    for _ in filler:
        pass

    @pl.when(s > 0)
    def _():
        below_copy.wait_send()

    for store in stores:
        store.wait()


def body(n_space, n_rep, stem_input, stem_preact, deep_cotangent, tissue_tiles, conv_weight, expand_weight):
    share = tissue_tiles.astype(F32) / TILES
    _, in_rows, cols, channels = stem_input.shape
    _, half_rows, width, _ = stem_preact.shape
    _, deep_rows, band, deep = deep_cotangent.shape
    devices = n_space * n_rep
    block = half_rows * band
    per_piece = max(2, -(-8 * devices // channels))
    piece_rows = padded_rows(per_piece * channels, devices)
    n_units = len(UNITS) + deep // channels
    n_pieces = -(-n_units // per_piece)
    all_rows = n_pieces * piece_rows
    grad_scale = float(n_rep * half_rows * n_space * width) ** (-0.5)
    sizes = layout(n_space, n_rep)
    copies = sum(n - 1 for n in sizes.values())
    anywhere = pl.BlockSpec(memory_space=pl.ANY)
    dma = pltpu.SemaphoreType.DMA
    grad_input, conv_sum, expand_sum = pl.pallas_call(
        functools.partial(kernel, n_space, n_rep, per_piece, piece_rows, grad_scale),
        out_shape=(
            jax.ShapeDtypeStruct((in_rows, cols, channels), BF16),
            jax.ShapeDtypeStruct((3, 3 * channels, channels), F32),
            jax.ShapeDtypeStruct((channels, deep), F32),
        ),
        in_specs=[
            pl.BlockSpec(memory_space=pltpu.SMEM),
            *[pl.BlockSpec(memory_space=pltpu.HBM)] * 5,
        ],
        out_specs=(anywhere, anywhere, anywhere),
        scratch_shapes=[
            pltpu.VMEM((in_rows, cols, channels), BF16),
            pltpu.VMEM(stem_preact.shape[1:], BF16),
            pltpu.VMEM((deep_rows * band, deep), BF16),
            pltpu.VMEM(conv_weight.shape, BF16),
            pltpu.VMEM(expand_weight.shape, BF16),
            pltpu.VMEM((deep_rows * band, deep), BF16),
            pltpu.VMEM((n_space, block, channels), BF16),
            pltpu.VMEM((n_space, block, channels), BF16),
            pltpu.VMEM((n_space, block, channels), BF16),
            pltpu.VMEM((n_space, block, channels), BF16),
            pltpu.VMEM((cols, cols), BF16),
            pltpu.VMEM((2, 2, channels, half_rows * width), BF16),
            pltpu.VMEM(((half_rows + 1) * width, channels), BF16),
            pltpu.VMEM(((half_rows + 1) * width, channels), BF16),
            pltpu.VMEM((width, channels), BF16),
            pltpu.VMEM((in_rows, cols, channels), BF16),
            pltpu.VMEM((2, half_rows * width, channels), BF16),
            pltpu.VMEM((all_rows, channels), F32),
            pltpu.VMEM((all_rows, channels), F32),
            pltpu.VMEM((all_rows, channels), F32),
            dma((5,)),
            dma((in_rows + n_units,)),
            dma((2, n_space)),
            dma((2, n_space)),
            dma((2,)),
            dma((n_pieces, copies)),
            dma((n_pieces, copies)),
            dma((n_pieces, copies)),
            dma((n_pieces, copies)),
        ],
        compiler_params=pltpu.CompilerParams(
            collective_id=0, has_side_effects=True, vmem_limit_bytes=VMEM_LIMIT
        ),
    )(
        share,
        stem_input[0],
        stem_preact[0],
        deep_cotangent.reshape(deep_rows * band, deep),
        conv_weight,
        expand_weight,
    )
    return (grad_input[None], conv_sum.reshape(3, 3, channels, channels), expand_sum)


def solution(mesh):
    return jax.shard_map(
        functools.partial(body, mesh.shape["space"], mesh.shape["rep"]),
        mesh=mesh,
        in_specs=(
            P("rep", "space", None, None),
            P("rep", "space", None, None),
            P("rep", None, "space", None),
            P("rep"),
            P(),
            P(),
        ),
        out_specs=(P("rep", "space", None, None), P(), P()),
        check_vma=False,
    )
```

```python
import functools
import heapq

import jax
import jax.numpy as jnp
from jax import lax
from jax.experimental import pallas as pl
from jax.experimental.pallas import tpu as pltpu
from jax.sharding import PartitionSpec as P

TILES = 64
VMEM_LIMIT = 32 * 1024 * 1024
F32, BF16 = jnp.float32, jnp.bfloat16
ORDERS = ("yxz", "xyz", "xyz", "yxz", "yxz", "zyx", "zxy", "yxz", "yxz", "yxz", "xyz", "xyz", "xyz")
UNITS = tuple((p, q) for p in (1, 2, 0) for q in range(3))


def dot(lhs, rhs, lhs_dim, rhs_dim):
    return lax.dot_general(
        lhs, rhs, (((lhs_dim,), (rhs_dim,)), ((), ())), preferred_element_type=F32
    )


def layout(n_space, n_rep):
    n_x = 2 if n_space % 2 == 0 else 1
    n_core = 2 if n_rep % 2 == 0 else 1
    return {"z": n_space // n_x, "x": n_x, "y": n_rep // n_core, "core": n_core}


def padded_rows(rows, n_devices):
    unit = 8 * n_devices
    return -(-rows // unit) * unit


def kernel(
    n_space, n_rep, per_piece, piece_rows, grad_scale,
    share_ref, x_hbm, pre_hbm, cot_hbm, cw_hbm, ew_hbm,
    gi_hbm, gc_hbm, ge_hbm,
    x_ref, pre_ref, cot_ref, cw_ref, ew_ref, weighted, hid_send, hid_recv, act_send, act_recv,
    spread, taps_in, grads, grads_next, below, gi_ref, mixed,
    acc, landing, total,
    load_sem, store_sem, hid_sems, act_sems, below_sems, rs_send, rs_recv, ag_send, ag_recv,
):
    s, r = lax.axis_index("space"), lax.axis_index("rep")
    sizes = layout(n_space, n_rep)
    n_x, n_core = sizes["x"], sizes["core"]
    here = {"z": s // n_x, "x": s % n_x, "y": r // n_core, "core": r % n_core}
    half_rows, width, channels = pre_ref.shape
    band = width // n_space
    block = half_rows * band

    def peer(axis, at):
        if axis == "z":
            return (at * n_x + here["x"], r)
        if axis == "x":
            return (here["z"] * n_x + at, r)
        if axis == "y":
            return (s, at * n_core + here["core"])
        return (s, here["y"] * n_core + at)

    pairs = ((cot_hbm, cot_ref), (ew_hbm, ew_ref), (pre_hbm, pre_ref), (x_hbm, x_ref), (cw_hbm, cw_ref))
    loads = [pltpu.make_async_copy(a, b, load_sem.at[k]) for k, (a, b) in enumerate(pairs)]
    load_cot, load_ew, load_pre, load_x, load_cw = loads
    for load in loads:
        load.start()

    barrier = pltpu.get_barrier_semaphore()
    partners = [((s + d) % n_space, r) for d in range(1, n_space)]
    for axis in ("y", "core"):
        partners += [peer(axis, (here[axis] + d) % sizes[axis]) for d in range(1, sizes[axis])]
    for partner in partners:
        pl.semaphore_signal(
            barrier, inc=1, device_id=partner, device_id_type=pl.DeviceIdType.MESH
        )

    load_cot.wait()
    weighted[...] = (cot_ref[...].astype(F32) * share_ref[0]).astype(BF16)
    load_ew.wait()
    hidden = dot(weighted[...], ew_ref[...], 1, 1).astype(BF16)
    for j in range(n_space):
        hid_send[j] = hidden[j * block : (j + 1) * block]
    load_pre.wait()
    for j in range(n_space):
        for i in range(half_rows):
            rows = pre_ref[i, j * band : (j + 1) * band, :].astype(F32)
            act_send[j, i * band : (i + 1) * band, :] = jnp.maximum(rows, 0.0).astype(BF16)
    pl.semaphore_wait(barrier, len(partners))

    def exchange(source, target, sems):
        copies = []
        for d in range(1, n_space):
            to = (s + d) % n_space
            copies.append(
                pltpu.make_async_remote_copy(
                    src_ref=source.at[to],
                    dst_ref=target.at[s],
                    send_sem=sems.at[0, d],
                    recv_sem=sems.at[1, d],
                    device_id=(to, r),
                    device_id_type=pl.DeviceIdType.MESH,
                )
            )
            copies[-1].start()
        target[s] = source[s]
        return copies

    hid_copies = exchange(hid_send, hid_recv, hid_sems)

    out_at = lax.broadcasted_iota(jnp.int32, (2 * width, 2 * width), 0)
    in_at = lax.broadcasted_iota(jnp.int32, (2 * width, 2 * width), 1)
    wanted = jnp.where(in_at < width, 2 * in_at, 2 * (in_at - width) + 1)
    spread[...] = jnp.where(out_at == wanted, 1.0, 0.0).astype(BF16)
    load_x.wait()
    for row in range(2 * half_rows):
        split = dot(x_ref[row], spread[...], 0, 0).astype(BF16)
        at = (row // 2) * width
        for parity in range(2):
            taps_in[row % 2, parity, :, at : at + width] = split[
                :, parity * width : (parity + 1) * width
            ]

    for copy in hid_copies:
        copy.wait()

    column = lax.broadcasted_iota(jnp.int32, (width, channels), 0)

    def put_grad(i, value):
        grads[i * width : (i + 1) * width, :] = value.astype(BF16)
        moved = jnp.where(column < width - 1, pltpu.roll(value, width - 1, 0), 0.0)
        grads_next[i * width : (i + 1) * width, :] = moved.astype(BF16)

    for i in range(half_rows):
        arrived = jnp.concatenate(
            [hid_recv[j, i * band : (i + 1) * band, :].astype(F32) for j in range(n_space)], axis=0
        )
        put_grad(i, jnp.where(pre_ref[i].astype(F32) > 0, arrived, 0.0))
    below_copy = pltpu.make_async_remote_copy(
        src_ref=grads.at[0:width],
        dst_ref=below,
        send_sem=below_sems.at[0],
        recv_sem=below_sems.at[1],
        device_id=((s + n_space - 1) % n_space, r),
        device_id_type=pl.DeviceIdType.MESH,
    )

    @pl.when(s > 0)
    def _():
        below_copy.start()

    act_copies = exchange(act_send, act_recv, act_sems)
    span = half_rows * width
    deep = weighted.shape[1]
    n_units = len(UNITS) + deep // channels
    n_pieces = -(-n_units // per_piece)

    def unit_row(unit):
        return unit // per_piece * piece_rows + unit % per_piece * channels

    def conv_unit(unit):
        row_tap, col_tap = UNITS[unit]
        first = width if row_tap == 0 else 0
        grad = grads_next if col_tap == 0 else grads
        at = unit_row(unit)
        acc[at : at + channels, :] = dot(
            taps_in[(row_tap + 1) % 2, (col_tap + 1) % 2], grad[first : first + span, :], 1, 0
        )

    def expand_units():
        for copy in act_copies:
            copy.wait()
        active = act_recv[...].astype(F32).reshape(n_space * block, channels).astype(BF16)
        for k in range(deep // channels):
            at = unit_row(len(UNITS) + k)
            acc[at : at + channels, :] = dot(
                active, weighted[:, k * channels : (k + 1) * channels], 0, 0
            )

    def low_units():
        @pl.when(s < n_space - 1)
        def _():
            below_copy.wait_recv()

        last = jnp.where(s < n_space - 1, 1.0, 0.0)
        put_grad(half_rows, jnp.where(last > 0.5, below[...].astype(F32), 0.0))
        for unit in range(6, 9):
            conv_unit(unit)

    def piece(k):
        base, length = k * piece_rows, piece_rows
        slot, sem = base, 0
        levels = []
        for axis in ("core",) + tuple(ORDERS[k % len(ORDERS)]):
            n, at = sizes[axis], here[axis]
            if n == 1:
                continue
            sub = length // n
            copies, slots = [], []
            for d in range(1, n):
                to = (at + d) % n
                copies.append(
                    pltpu.make_async_remote_copy(
                        src_ref=acc.at[pl.ds(pl.multiple_of(base + to * sub, 8), sub)],
                        dst_ref=landing.at[pl.ds(slot, sub)],
                        send_sem=rs_send.at[k, sem],
                        recv_sem=rs_recv.at[k, sem],
                        device_id=peer(axis, to),
                        device_id_type=pl.DeviceIdType.MESH,
                    )
                )
                copies[-1].start()
                slots.append(slot)
                slot += sub
                sem += 1
            yield axis, sub
            for copy in copies:
                copy.wait()
            base = base + at * sub
            own = pl.ds(pl.multiple_of(base, 8), sub)
            value = acc[own, :]
            for place in slots:
                value = value + landing[place : place + sub, :]
            acc[own, :] = value
            length = sub
            levels.append((axis, n, at, base, sub))
        total[own, :] = value * grad_scale
        sem = 0
        for axis, n, at, base, sub in reversed(levels):
            copies = []
            mine = total.at[pl.ds(pl.multiple_of(base, 8), sub)]
            for d in range(1, n):
                copies.append(
                    pltpu.make_async_remote_copy(
                        src_ref=mine,
                        dst_ref=mine,
                        send_sem=ag_send.at[k, sem],
                        recv_sem=ag_recv.at[k, sem],
                        device_id=peer(axis, (at + d) % n),
                        device_id_type=pl.DeviceIdType.MESH,
                    )
                )
                copies[-1].start()
                sem += 1
            yield axis, sub
            for copy in copies:
                copy.wait()
        for unit in range(k * per_piece, min((k + 1) * per_piece, n_units)):
            rows = total.at[pl.ds(unit_row(unit), channels)]
            if unit < len(UNITS):
                p, q = UNITS[unit]
                target = gc_hbm.at[p, pl.ds(q * channels, channels)]
            else:
                target = ge_hbm.at[:, pl.ds((unit - len(UNITS)) * channels, channels)]
            stores.append(
                pltpu.make_async_copy(rows, target, store_sem.at[2 * half_rows + unit])
            )
            stores[-1].start()

    def term(first, row_tap, col_tap):
        grad = grads_next if col_tap == 0 else grads
        return dot(grad[first : first + span, :], cw_ref[row_tap, col_tap], 1, 1)

    def input_parts():
        load_cw.wait()
        for row_parity in range(2):
            pairs = [(0, 1)] if row_parity == 0 else [(0, 2), (width, 0)]
            for parity in range(2):
                cols = (1,) if parity == 0 else (2, 0)
                terms = [term(first, p, q) for first, p in pairs for q in cols]
                mixed[parity] = functools.reduce(jnp.add, terms).astype(BF16)
                yield
            for i in range(half_rows):
                both = jnp.concatenate(
                    [mixed[parity, i * width : (i + 1) * width, :] for parity in range(2)], axis=0
                )
                row = 2 * i + row_parity
                gi_ref[row] = dot(spread[...], both, 1, 0).astype(BF16)
                stores.append(
                    pltpu.make_async_copy(gi_ref.at[row], gi_hbm.at[row], store_sem.at[row])
                )
                stores[-1].start()
                yield

    stores = []
    pieces = [piece(k) for k in range(n_pieces)]
    filler = input_parts()
    line_free = dict.fromkeys(sizes, 0.0)
    line_cost = {"core": 1 / 6, "x": 2.0, "y": 2.0, "z": 2.0 * (sizes["z"] // 2) ** 2}
    per_row = channels * 4e-5
    done_units = set()
    begun = set()
    events = []
    clock = 0.0

    def advance(k):
        stage = next(pieces[k], None)
        if stage is not None:
            axis, sub = stage
            begin = max(clock, line_free[axis])
            line_free[axis] = begin + sub * per_row * line_cost[axis]
            heapq.heappush(events, (line_free[axis] + 1.5, 2, k))

    def ready(units):
        done_units.update(units)
        for k in range(n_pieces):
            members = range(k * per_piece, min((k + 1) * per_piece, n_units))
            if k not in begun and done_units.issuperset(members):
                begun.add(k)
                used = len(members) * channels
                if used < piece_rows:
                    acc[k * piece_rows + used : (k + 1) * piece_rows, :] = jnp.zeros(
                        (piece_rows - used, channels), F32
                    )
                advance(k)

    heapq.heappush(events, (4.0, 0, 0))
    heapq.heappush(events, (7.0, 1, 0))
    for unit in range(6):
        conv_unit(unit)
        ready([unit])
        clock += 0.2
    low_done = False
    while events:
        while low_done and events[0][0] > clock + 0.3 and next(filler, "end") != "end":
            clock += 0.4
        when, kind, k = heapq.heappop(events)
        clock = max(clock, when)
        if kind == 0:
            low_units()
            low_done = True
            ready([6, 7, 8])
            clock += 0.6
        elif kind == 1:
            expand_units()
            ready(range(len(UNITS), n_units))
            clock += 0.8
        else:
            advance(k)
            clock += 0.1
    for _ in filler:
        pass

    @pl.when(s > 0)
    def _():
        below_copy.wait_send()

    for store in stores:
        store.wait()


def body(n_space, n_rep, stem_input, stem_preact, deep_cotangent, tissue_tiles, conv_weight, expand_weight):
    share = tissue_tiles.astype(F32) / TILES
    _, in_rows, cols, channels = stem_input.shape
    _, half_rows, width, _ = stem_preact.shape
    _, deep_rows, band, deep = deep_cotangent.shape
    devices = n_space * n_rep
    block = half_rows * band
    per_piece = -(-8 * devices // channels)
    piece_rows = padded_rows(per_piece * channels, devices)
    n_units = len(UNITS) + deep // channels
    n_pieces = -(-n_units // per_piece)
    all_rows = n_pieces * piece_rows
    grad_scale = float(n_rep * half_rows * n_space * width) ** (-0.5)
    sizes = layout(n_space, n_rep)
    copies = sum(n - 1 for n in sizes.values())
    anywhere = pl.BlockSpec(memory_space=pl.ANY)
    dma = pltpu.SemaphoreType.DMA
    grad_input, conv_sum, expand_sum = pl.pallas_call(
        functools.partial(kernel, n_space, n_rep, per_piece, piece_rows, grad_scale),
        out_shape=(
            jax.ShapeDtypeStruct((in_rows, cols, channels), BF16),
            jax.ShapeDtypeStruct((3, 3 * channels, channels), F32),
            jax.ShapeDtypeStruct((channels, deep), F32),
        ),
        in_specs=[
            pl.BlockSpec(memory_space=pltpu.SMEM),
            *[pl.BlockSpec(memory_space=pltpu.HBM)] * 5,
        ],
        out_specs=(anywhere, anywhere, anywhere),
        scratch_shapes=[
            pltpu.VMEM((in_rows, cols, channels), BF16),
            pltpu.VMEM(stem_preact.shape[1:], BF16),
            pltpu.VMEM((deep_rows * band, deep), BF16),
            pltpu.VMEM(conv_weight.shape, BF16),
            pltpu.VMEM(expand_weight.shape, BF16),
            pltpu.VMEM((deep_rows * band, deep), BF16),
            pltpu.VMEM((n_space, block, channels), BF16),
            pltpu.VMEM((n_space, block, channels), BF16),
            pltpu.VMEM((n_space, block, channels), BF16),
            pltpu.VMEM((n_space, block, channels), BF16),
            pltpu.VMEM((cols, cols), BF16),
            pltpu.VMEM((2, 2, channels, half_rows * width), BF16),
            pltpu.VMEM(((half_rows + 1) * width, channels), BF16),
            pltpu.VMEM(((half_rows + 1) * width, channels), BF16),
            pltpu.VMEM((width, channels), BF16),
            pltpu.VMEM((in_rows, cols, channels), BF16),
            pltpu.VMEM((2, half_rows * width, channels), BF16),
            pltpu.VMEM((all_rows, channels), F32),
            pltpu.VMEM((all_rows, channels), F32),
            pltpu.VMEM((all_rows, channels), F32),
            dma((5,)),
            dma((in_rows + n_units,)),
            dma((2, n_space)),
            dma((2, n_space)),
            dma((2,)),
            dma((n_pieces, copies)),
            dma((n_pieces, copies)),
            dma((n_pieces, copies)),
            dma((n_pieces, copies)),
        ],
        compiler_params=pltpu.CompilerParams(
            collective_id=0, has_side_effects=True, vmem_limit_bytes=VMEM_LIMIT
        ),
    )(
        share,
        stem_input[0],
        stem_preact[0],
        deep_cotangent.reshape(deep_rows * band, deep),
        conv_weight,
        expand_weight,
    )
    return (grad_input[None], conv_sum.reshape(3, 3, channels, channels), expand_sum)


def solution(mesh):
    return jax.shard_map(
        functools.partial(body, mesh.shape["space"], mesh.shape["rep"]),
        mesh=mesh,
        in_specs=(
            P("rep", "space", None, None),
            P("rep", "space", None, None),
            P("rep", None, "space", None),
            P("rep"),
            P(),
            P(),
        ),
        out_specs=(P("rep", "space", None, None), P(), P()),
        check_vma=False,
    )
```

```python
import functools
import heapq

import jax
import jax.numpy as jnp
from jax import lax
from jax.experimental import pallas as pl
from jax.experimental.pallas import tpu as pltpu
from jax.sharding import PartitionSpec as P

TILES = 64
VMEM_LIMIT = 32 * 1024 * 1024
F32, BF16 = jnp.float32, jnp.bfloat16
ORDERS = ("yxz", "xyz", "xyz", "yxz", "yxz", "zyx", "zxy", "yxz", "yxz", "yxz", "xyz", "xyz", "xyz")
UNITS = tuple((p, q) for p in (1, 2, 0) for q in range(3))


def dot(lhs, rhs, lhs_dim, rhs_dim):
    return lax.dot_general(
        lhs, rhs, (((lhs_dim,), (rhs_dim,)), ((), ())), preferred_element_type=F32
    )


def layout(n_space, n_rep):
    n_x = 2 if n_space % 2 == 0 else 1
    n_core = 2 if n_rep % 2 == 0 else 1
    return {"z": n_space // n_x, "x": n_x, "y": n_rep // n_core, "core": n_core}


def padded_rows(rows, n_devices):
    unit = 8 * n_devices
    return -(-rows // unit) * unit


def kernel(
    n_space, n_rep, per_piece, piece_rows, grad_scale,
    x_hbm, pre_hbm, cot_hbm, cw_hbm, ew_hbm,
    gi_hbm, gc_hbm, ge_hbm,
    x_ref, pre_ref, cw_ref, ew_ref, weighted, hid_send, hid_recv, act_send, act_recv,
    spread, taps_in, grads, grads_next, below, gi_ref, mixed,
    acc, landing, total,
    load_sem, store_sem, hid_sems, act_sems, below_sems, rs_send, rs_recv, ag_send, ag_recv,
):
    s, r = lax.axis_index("space"), lax.axis_index("rep")
    sizes = layout(n_space, n_rep)
    n_x, n_core = sizes["x"], sizes["core"]
    here = {"z": s // n_x, "x": s % n_x, "y": r // n_core, "core": r % n_core}
    half_rows, width, channels = pre_ref.shape
    band = width // n_space
    block = half_rows * band

    def peer(axis, at):
        if axis == "z":
            return (at * n_x + here["x"], r)
        if axis == "x":
            return (here["z"] * n_x + at, r)
        if axis == "y":
            return (s, at * n_core + here["core"])
        return (s, here["y"] * n_core + at)

    pairs = ((cot_hbm, weighted), (ew_hbm, ew_ref), (pre_hbm, pre_ref), (x_hbm, x_ref), (cw_hbm, cw_ref))
    loads = [pltpu.make_async_copy(a, b, load_sem.at[k]) for k, (a, b) in enumerate(pairs)]
    load_cot, load_ew, load_pre, load_x, load_cw = loads
    for load in loads:
        load.start()

    barrier = pltpu.get_barrier_semaphore()
    partners = [((s + d) % n_space, r) for d in range(1, n_space)]
    for axis in ("y", "core"):
        partners += [peer(axis, (here[axis] + d) % sizes[axis]) for d in range(1, sizes[axis])]
    for partner in partners:
        pl.semaphore_signal(
            barrier, inc=1, device_id=partner, device_id_type=pl.DeviceIdType.MESH
        )

    load_cot.wait()
    load_ew.wait()
    hidden = dot(weighted[...], ew_ref[...], 1, 1).astype(BF16)
    for j in range(n_space):
        hid_send[j] = hidden[j * block : (j + 1) * block]
    load_pre.wait()
    for j in range(n_space):
        for i in range(half_rows):
            rows = pre_ref[i, j * band : (j + 1) * band, :].astype(F32)
            act_send[j, i * band : (i + 1) * band, :] = jnp.maximum(rows, 0.0).astype(BF16)
    pl.semaphore_wait(barrier, len(partners))

    def exchange(source, target, sems):
        copies = []
        for d in range(1, n_space):
            to = (s + d) % n_space
            copies.append(
                pltpu.make_async_remote_copy(
                    src_ref=source.at[to],
                    dst_ref=target.at[s],
                    send_sem=sems.at[0, d],
                    recv_sem=sems.at[1, d],
                    device_id=(to, r),
                    device_id_type=pl.DeviceIdType.MESH,
                )
            )
            copies[-1].start()
        target[s] = source[s]
        return copies

    hid_copies = exchange(hid_send, hid_recv, hid_sems)

    out_at = lax.broadcasted_iota(jnp.int32, (2 * width, 2 * width), 0)
    in_at = lax.broadcasted_iota(jnp.int32, (2 * width, 2 * width), 1)
    wanted = jnp.where(in_at < width, 2 * in_at, 2 * (in_at - width) + 1)
    spread[...] = jnp.where(out_at == wanted, 1.0, 0.0).astype(BF16)
    load_x.wait()
    for row in range(2 * half_rows):
        split = dot(x_ref[row], spread[...], 0, 0).astype(BF16)
        at = (row // 2) * width
        for parity in range(2):
            taps_in[row % 2, parity, :, at : at + width] = split[
                :, parity * width : (parity + 1) * width
            ]

    for copy in hid_copies:
        copy.wait()

    column = lax.broadcasted_iota(jnp.int32, (width, channels), 0)

    def put_grad(i, value):
        grads[i * width : (i + 1) * width, :] = value.astype(BF16)
        moved = jnp.where(column < width - 1, pltpu.roll(value, width - 1, 0), 0.0)
        grads_next[i * width : (i + 1) * width, :] = moved.astype(BF16)

    for i in range(half_rows):
        arrived = jnp.concatenate(
            [hid_recv[j, i * band : (i + 1) * band, :].astype(F32) for j in range(n_space)], axis=0
        )
        put_grad(i, jnp.where(pre_ref[i].astype(F32) > 0, arrived, 0.0))
    below_copy = pltpu.make_async_remote_copy(
        src_ref=grads.at[0:width],
        dst_ref=below,
        send_sem=below_sems.at[0],
        recv_sem=below_sems.at[1],
        device_id=((s + n_space - 1) % n_space, r),
        device_id_type=pl.DeviceIdType.MESH,
    )

    @pl.when(s > 0)
    def _():
        below_copy.start()

    act_copies = exchange(act_send, act_recv, act_sems)
    span = half_rows * width
    deep = weighted.shape[1]
    n_units = len(UNITS) + deep // channels
    n_pieces = -(-n_units // per_piece)

    def unit_row(unit):
        return unit // per_piece * piece_rows + unit % per_piece * channels

    def conv_unit(unit):
        row_tap, col_tap = UNITS[unit]
        first = width if row_tap == 0 else 0
        grad = grads_next if col_tap == 0 else grads
        at = unit_row(unit)
        acc[at : at + channels, :] = dot(
            taps_in[(row_tap + 1) % 2, (col_tap + 1) % 2], grad[first : first + span, :], 1, 0
        )

    def expand_units():
        for copy in act_copies:
            copy.wait()
        active = act_recv[...].astype(F32).reshape(n_space * block, channels).astype(BF16)
        for k in range(deep // channels):
            at = unit_row(len(UNITS) + k)
            acc[at : at + channels, :] = dot(
                active, weighted[:, k * channels : (k + 1) * channels], 0, 0
            )

    def low_units():
        @pl.when(s < n_space - 1)
        def _():
            below_copy.wait_recv()

        last = jnp.where(s < n_space - 1, 1.0, 0.0)
        put_grad(half_rows, jnp.where(last > 0.5, below[...].astype(F32), 0.0))
        for unit in range(6, 9):
            conv_unit(unit)

    def piece(k):
        base, length = k * piece_rows, piece_rows
        slot, sem = base, 0
        levels = []
        for axis in ("core",) + tuple(ORDERS[k % len(ORDERS)]):
            n, at = sizes[axis], here[axis]
            if n == 1:
                continue
            sub = length // n
            copies, slots = [], []
            for d in range(1, n):
                to = (at + d) % n
                copies.append(
                    pltpu.make_async_remote_copy(
                        src_ref=acc.at[pl.ds(pl.multiple_of(base + to * sub, 8), sub)],
                        dst_ref=landing.at[pl.ds(slot, sub)],
                        send_sem=rs_send.at[k, sem],
                        recv_sem=rs_recv.at[k, sem],
                        device_id=peer(axis, to),
                        device_id_type=pl.DeviceIdType.MESH,
                    )
                )
                copies[-1].start()
                slots.append(slot)
                slot += sub
                sem += 1
            yield axis, sub
            for copy in copies:
                copy.wait()
            base = base + at * sub
            own = pl.ds(pl.multiple_of(base, 8), sub)
            value = acc[own, :]
            for place in slots:
                value = value + landing[place : place + sub, :]
            acc[own, :] = value
            length = sub
            levels.append((axis, n, at, base, sub))
        total[own, :] = value * grad_scale
        sem = 0
        for axis, n, at, base, sub in reversed(levels):
            copies = []
            mine = total.at[pl.ds(pl.multiple_of(base, 8), sub)]
            for d in range(1, n):
                copies.append(
                    pltpu.make_async_remote_copy(
                        src_ref=mine,
                        dst_ref=mine,
                        send_sem=ag_send.at[k, sem],
                        recv_sem=ag_recv.at[k, sem],
                        device_id=peer(axis, (at + d) % n),
                        device_id_type=pl.DeviceIdType.MESH,
                    )
                )
                copies[-1].start()
                sem += 1
            yield axis, sub
            for copy in copies:
                copy.wait()
        for unit in range(k * per_piece, min((k + 1) * per_piece, n_units)):
            rows = total.at[pl.ds(unit_row(unit), channels)]
            if unit < len(UNITS):
                p, q = UNITS[unit]
                target = gc_hbm.at[p, pl.ds(q * channels, channels)]
            else:
                target = ge_hbm.at[:, pl.ds((unit - len(UNITS)) * channels, channels)]
            stores.append(
                pltpu.make_async_copy(rows, target, store_sem.at[2 * half_rows + unit])
            )
            stores[-1].start()

    def term(first, row_tap, col_tap):
        grad = grads_next if col_tap == 0 else grads
        return dot(grad[first : first + span, :], cw_ref[row_tap, col_tap], 1, 1)

    def input_parts():
        load_cw.wait()
        for row_parity in range(2):
            pairs = [(0, 1)] if row_parity == 0 else [(0, 2), (width, 0)]
            for parity in range(2):
                cols = (1,) if parity == 0 else (2, 0)
                terms = [term(first, p, q) for first, p in pairs for q in cols]
                mixed[parity] = functools.reduce(jnp.add, terms).astype(BF16)
                yield
            for i in range(half_rows):
                both = jnp.concatenate(
                    [mixed[parity, i * width : (i + 1) * width, :] for parity in range(2)], axis=0
                )
                row = 2 * i + row_parity
                gi_ref[row] = dot(spread[...], both, 1, 0).astype(BF16)
                stores.append(
                    pltpu.make_async_copy(gi_ref.at[row], gi_hbm.at[row], store_sem.at[row])
                )
                stores[-1].start()
                yield

    stores = []
    pieces = [piece(k) for k in range(n_pieces)]
    filler = input_parts()
    line_free = dict.fromkeys(sizes, 0.0)
    line_cost = {"core": 1 / 6, "x": 2.0, "y": 2.0, "z": 2.0 * (sizes["z"] // 2) ** 2}
    per_row = channels * 4e-5
    done_units = set()
    begun = set()
    events = []
    clock = 0.0

    def advance(k):
        stage = next(pieces[k], None)
        if stage is not None:
            axis, sub = stage
            begin = max(clock, line_free[axis])
            line_free[axis] = begin + sub * per_row * line_cost[axis]
            heapq.heappush(events, (line_free[axis] + 1.5, 2, k))

    def ready(units):
        done_units.update(units)
        for k in range(n_pieces):
            members = range(k * per_piece, min((k + 1) * per_piece, n_units))
            if k not in begun and done_units.issuperset(members):
                begun.add(k)
                used = len(members) * channels
                if used < piece_rows:
                    acc[k * piece_rows + used : (k + 1) * piece_rows, :] = jnp.zeros(
                        (piece_rows - used, channels), F32
                    )
                advance(k)

    heapq.heappush(events, (4.0, 0, 0))
    heapq.heappush(events, (7.0, 1, 0))
    for unit in range(6):
        conv_unit(unit)
        ready([unit])
        clock += 0.2
    low_done = False
    while events:
        while low_done and events[0][0] > clock + 0.3 and next(filler, "end") != "end":
            clock += 0.4
        when, kind, k = heapq.heappop(events)
        clock = max(clock, when)
        if kind == 0:
            low_units()
            low_done = True
            ready([6, 7, 8])
            clock += 0.6
        elif kind == 1:
            expand_units()
            ready(range(len(UNITS), n_units))
            clock += 0.8
        else:
            advance(k)
            clock += 0.1
    for _ in filler:
        pass

    @pl.when(s > 0)
    def _():
        below_copy.wait_send()

    for store in stores:
        store.wait()


def body(n_space, n_rep, stem_input, stem_preact, deep_cotangent, tissue_tiles, conv_weight, expand_weight):
    share = tissue_tiles.astype(F32) / TILES
    weighted = (deep_cotangent.astype(F32) * share[:, None, None, None]).astype(BF16)
    _, in_rows, cols, channels = stem_input.shape
    _, half_rows, width, _ = stem_preact.shape
    _, deep_rows, band, deep = deep_cotangent.shape
    devices = n_space * n_rep
    block = half_rows * band
    per_piece = -(-8 * devices // channels)
    piece_rows = padded_rows(per_piece * channels, devices)
    n_units = len(UNITS) + deep // channels
    n_pieces = -(-n_units // per_piece)
    all_rows = n_pieces * piece_rows
    grad_scale = float(n_rep * half_rows * n_space * width) ** (-0.5)
    sizes = layout(n_space, n_rep)
    copies = sum(n - 1 for n in sizes.values())
    anywhere = pl.BlockSpec(memory_space=pl.ANY)
    dma = pltpu.SemaphoreType.DMA
    grad_input, conv_sum, expand_sum = pl.pallas_call(
        functools.partial(kernel, n_space, n_rep, per_piece, piece_rows, grad_scale),
        out_shape=(
            jax.ShapeDtypeStruct((in_rows, cols, channels), BF16),
            jax.ShapeDtypeStruct((3, 3 * channels, channels), F32),
            jax.ShapeDtypeStruct((channels, deep), F32),
        ),
        in_specs=[
            *[pl.BlockSpec(memory_space=pltpu.HBM)] * 5,
        ],
        out_specs=(anywhere, anywhere, anywhere),
        scratch_shapes=[
            pltpu.VMEM((in_rows, cols, channels), BF16),
            pltpu.VMEM(stem_preact.shape[1:], BF16),
            pltpu.VMEM(conv_weight.shape, BF16),
            pltpu.VMEM(expand_weight.shape, BF16),
            pltpu.VMEM((deep_rows * band, deep), BF16),
            pltpu.VMEM((n_space, block, channels), BF16),
            pltpu.VMEM((n_space, block, channels), BF16),
            pltpu.VMEM((n_space, block, channels), BF16),
            pltpu.VMEM((n_space, block, channels), BF16),
            pltpu.VMEM((cols, cols), BF16),
            pltpu.VMEM((2, 2, channels, half_rows * width), BF16),
            pltpu.VMEM(((half_rows + 1) * width, channels), BF16),
            pltpu.VMEM(((half_rows + 1) * width, channels), BF16),
            pltpu.VMEM((width, channels), BF16),
            pltpu.VMEM((in_rows, cols, channels), BF16),
            pltpu.VMEM((2, half_rows * width, channels), BF16),
            pltpu.VMEM((all_rows, channels), F32),
            pltpu.VMEM((all_rows, channels), F32),
            pltpu.VMEM((all_rows, channels), F32),
            dma((5,)),
            dma((in_rows + n_units,)),
            dma((2, n_space)),
            dma((2, n_space)),
            dma((2,)),
            dma((n_pieces, copies)),
            dma((n_pieces, copies)),
            dma((n_pieces, copies)),
            dma((n_pieces, copies)),
        ],
        compiler_params=pltpu.CompilerParams(
            collective_id=0, has_side_effects=True, vmem_limit_bytes=VMEM_LIMIT
        ),
    )(
        stem_input[0],
        stem_preact[0],
        weighted.reshape(deep_rows * band, deep),
        conv_weight,
        expand_weight,
    )
    return (grad_input[None], conv_sum.reshape(3, 3, channels, channels), expand_sum)


def solution(mesh):
    return jax.shard_map(
        functools.partial(body, mesh.shape["space"], mesh.shape["rep"]),
        mesh=mesh,
        in_specs=(
            P("rep", "space", None, None),
            P("rep", "space", None, None),
            P("rep", None, "space", None),
            P("rep"),
            P(),
            P(),
        ),
        out_specs=(P("rep", "space", None, None), P(), P()),
        check_vma=False,
    )
```
